1024 devices in a mesh: win: 4 (over x), lat: 16 (over z_hi, y, core), lon: 16 (over z_lo).
Axes of the slice: x: 4, y: 4, z: 32 (z_hi: 2, z_lo: 16; z = z_hi * 16 + z_lo), core: 2. Of those that a mesh axis runs over, the one named last changes fastest.
Arguments:
- increment: float32 [4, 3, 1024, 4096], P('win', None, 'lat', 'lon'), may hold values from -6 to 6
- model_weight: float32 [4, 3, 1024, 4096], P('win', None, 'lat', 'lon'), may hold values from 0.25 to 4
- winds: float32 [4, 2, 1024, 4096], P('win', None, 'lat', 'lon'), may hold values from -0.3 to 0.3
- reaction: float32 [4, 3, 3], P('win'), may hold values from -1 to 1
- obs_cells: int32 [4, 16, 16, 1024], P('win', 'lat', 'lon'), may hold values from 0 to 16383
- obs_weight: float32 [4, 3, 16, 16, 1024], P('win', None, 'lat', 'lon'), may hold values from 0.5 to 8
Outputs:
- hess_vec: float32 [4, 3, 1024, 4096], P('win', None, 'lat', 'lon')
The draws below stay inside these ranges and needn't reach their ends.
Inputs may be any that keep to these rules, and one draw needn't show every extreme that they name: `obs_cells`: an index row * 256 + column within its tile.
All inputs are finite; a program needn't handle non-finite values.
Results may differ from the reference program's by a relative error of at most 0.00002.
Values sent between devices are 32-bit elements; how exact they have to be, the bound alone decides.
A program may use at most 64 MiB of HBM per device.

```python
import math
import jax
import jax.numpy as jnp

FIELDS = 3
CLAT = 64
CLON = 256
NOBS = 1024
WINDOWS = 4
LAT_TILES = 16
LON_TILES = 16
NLAT = 1024
NLON = 4096


def set_ends(values, stream_key, smallest, largest):
    dims = values.shape
    index_at = [jax.random.randint(jax.random.fold_in(stream_key, axis), (), 0, dims[axis]) for axis in range(len(dims))]
    values = values.at[tuple(index_at)].set(smallest)
    longest = dims.index(max(dims))
    index_at[longest] = (index_at[longest] + 1) % dims[longest]
    return values.at[tuple(index_at)].set(largest)


def levels(own_key, extent, cuts, low, high):
    gain = 1.0
    for dim, shards_of in cuts:
        draws = jax.random.uniform(jax.random.fold_in(jax.random.fold_in(own_key, 6), dim), (shards_of,), jnp.float32, low / len(cuts), high / len(cuts))
        gain = gain * jnp.repeat(jnp.exp(draws), extent[dim] // shards_of).reshape((-1,) + (1,) * (len(extent) - 1 - dim))
    return gain


def scatter_about(rng, extent, width, bound, shards=(), dtype=jnp.bfloat16):
    level = levels(rng, extent, shards, -0.22, 0.18) if shards else 1.0
    values = jax.random.normal(rng, extent, jnp.float32) * width * level
    return jnp.minimum(jnp.maximum(values, -bound), bound).astype(dtype)


def setup_inputs(seed: int = 0) -> dict:
    key_of = jax.random.split(jax.random.key(seed), 7)
    return {
        "increment": scatter_about(key_of[0], (WINDOWS, FIELDS, NLAT, NLON), 1.0, 6.0, ((0, 4), (2, 16), (3, 16)), jnp.float32),
        "model_weight": jnp.clip(jnp.exp(math.log(4.0) - 2.7725887 * jax.random.uniform(key_of[1], (WINDOWS, FIELDS, NLAT, NLON), jnp.float32) ** levels(key_of[1], (WINDOWS, FIELDS, NLAT, NLON), ((0, 4), (2, 16), (3, 16)), -0.2, 0.2)), 0.25, 4.0),
        "winds": jnp.clip(jax.random.uniform(key_of[2], (WINDOWS, 2, NLAT, NLON), jnp.float32, -0.3, 0.3) * levels(key_of[2], (WINDOWS, 2, NLAT, NLON), ((0, 4), (2, 16), (3, 16)), -0.4, 0.0), -0.3, 0.3),
        "reaction": scatter_about(key_of[3], (WINDOWS, FIELDS, FIELDS), 0.2, 1.0, ((0, 4),), jnp.float32),
        "obs_cells": set_ends(jax.random.randint(key_of[4], (WINDOWS, LAT_TILES, LON_TILES, NOBS), 0, CLAT * CLON), jax.random.fold_in(key_of[4], 1), 0, (CLAT * CLON) - 1).astype(jnp.int32),
        "obs_weight": jnp.clip(jnp.exp(math.log(8.0) - 2.7725887 * jax.random.uniform(key_of[5], (WINDOWS, FIELDS, LAT_TILES, LON_TILES, NOBS), jnp.float32) ** levels(key_of[5], (WINDOWS, FIELDS, LAT_TILES, LON_TILES, NOBS), ((0, 4), (2, 16), (3, 16)), -0.2, 0.2)), 0.5, 8.0),
    }


DIFFUSION = 0.15


def neighbours(field):
    padded = jnp.pad(field, ((0, 0), (1, 1), (0, 0)))
    north_side = padded[:, 2:, :]
    south_side = padded[:, :-2, :]
    east_side = jnp.roll(field, -1, axis=2)
    west_side = jnp.roll(field, 1, axis=2)
    return north_side, south_side, east_side, west_side


def mixing(reaction, field):
    return jnp.sum(reaction[:, :, None, None] * field[None], axis=1)


def tangent_step(field, winds, reaction):
    north_side, south_side, east_side, west_side = neighbours(field)
    spread = north_side + south_side + east_side + west_side
    result = (1.0 - 4.0 * DIFFUSION) * field + DIFFUSION * spread
    result = result - winds[0] * (east_side - west_side) - winds[1] * (north_side - south_side)
    return result + mixing(reaction, field)


def adjoint_step(field, winds, reaction):
    north_side, south_side, east_side, west_side = neighbours(field)
    spread = north_side + south_side + east_side + west_side
    lon_flux = neighbours(winds[0] * field)
    lat_flux = neighbours(winds[1] * field)
    result = (1.0 - 4.0 * DIFFUSION) * field + DIFFUSION * spread
    result = result + (lon_flux[2] - lon_flux[3]) + (lat_flux[0] - lat_flux[1])
    return result + mixing(reaction.T, field)


def observe(state, row_ids, column_ids, weight):
    picked = state[:, row_ids, column_ids]
    return jnp.zeros_like(state).at[:, row_ids, column_ids].add(weight * picked)


def reference(increment, model_weight, winds, reaction, obs_cells, obs_weight):
    def forward_pair(field, wind_now, mixer):
        return tangent_step(tangent_step(field, wind_now, mixer), wind_now, mixer)

    def adjoint_pair(field, wind_now, mixer):
        return adjoint_step(adjoint_step(field, wind_now, mixer), wind_now, mixer)

    forward = jax.vmap(forward_pair)(increment, winds, reaction)
    earlier = jnp.concatenate([jnp.zeros_like(forward[:1]), forward[:-1]], axis=0)
    jump = model_weight * (increment - earlier)
    later = jnp.concatenate([jump[1:], jnp.zeros_like(jump[:1])], axis=0)
    lat_base = (jnp.arange(LAT_TILES) * CLAT).astype(jnp.int32)
    lon_base = (jnp.arange(LON_TILES) * CLON).astype(jnp.int32)
    rows = (lat_base[None, :, None, None] + obs_cells // CLON).astype(jnp.int32)
    columns = (lon_base[None, None, :, None] + obs_cells % CLON).astype(jnp.int32)
    observed = jax.vmap(observe)(forward, rows, columns, obs_weight)
    source = observed - later
    back = jax.vmap(adjoint_pair)(source, winds, reaction)
    return jump + back
```

```python
import functools

import jax
import jax.numpy as jnp
from jax import lax
from jax.experimental import pallas as pl
from jax.experimental.pallas import tpu as pltpu
from jax.sharding import PartitionSpec as P

DIFFUSION = 0.15
KEEP = 1.0 - 4.0 * DIFFUSION
MESH = pl.DeviceIdType.MESH
F32 = jnp.float32
BF16 = jnp.bfloat16
DIRS = ((1, 0), (-1, 0), (0, 1), (0, -1), (1, 1), (1, -1), (-1, 1), (-1, -1))


def rolled(x, shift, axis):
    shift = shift % x.shape[axis]
    return x if shift == 0 else pltpu.roll(x, shift, axis)


def east(x):
    return rolled(x, -1, 1)


def west(x):
    return rolled(x, 1, 1)


def north(x):
    return rolled(x, -1, 0)


def south(x):
    return rolled(x, 1, 0)


def tangent(xs, coef, mix):
    a, b, c, d = coef
    out = []
    for f in range(3):
        x = xs[f]
        y = a * east(x) + b * west(x) + c * north(x) + d * south(x)
        out.append(y + mix[f][0] * xs[0] + mix[f][1] * xs[1] + mix[f][2] * xs[2])
    return out


def adjoint(zs, coef, mix):
    a, b, c, d = coef
    out = []
    for f in range(3):
        z = zs[f]
        y = east(b * z) + west(a * z) + north(d * z) + south(c * z)
        out.append(y + mix[0][f] * zs[0] + mix[1][f] * zs[1] + mix[2][f] * zs[2])
    return out


def iota(shape, axis):
    return lax.broadcasted_iota(jnp.int32, shape, axis)


def kernel(
    sizes,
    inc_h, mw_h, winds_h, rea_h, cells_h, ow_h,
    out_ref,
    x_ext, u_ext, w_ext, coef, g_ext, h_ext, t_ext,
    mw_v, rea_s, cells_v, ow_v,
    pack, ce, cw, rows_own, rows_far, fwd0, ring_r, ring_c,
    got_rows_own, got_rows_far, got_cols, got_corner, inc_n, mw_n, got_fwd, got_ring_r, got_ring_c,
    load_sem, send_sem, recv_sem, xsend_sem, xrecv_sem,
):
    n_win, n_lat, n_lon = sizes
    win, lat, lon = lax.axis_index("win"), lax.axis_index("lat"), lax.axis_index("lon")
    R, C = 64, 256

    def lon_at(step):
        return lax.rem(lon + step + n_lon, n_lon)

    def lat_ok(step):
        return (lat + step >= 0) & (lat + step < n_lat)

    has_prev, has_next = win > 0, win < n_win - 1

    barrier = pltpu.get_barrier_semaphore()

    def tell(ok, target):
        @pl.when(ok)
        def _():
            pl.semaphore_signal(barrier, inc=1, device_id=target, device_id_type=MESH)

    for dlat, dlon in DIRS:
        tell(lat_ok(-dlat), (win, lat - dlat, lon_at(-dlon)))
        tell(has_next & lat_ok(-dlat), (win + 1, lat - dlat, lon_at(-dlon)))
    tell(has_next, (win + 1, lat, lon))
    tell(has_prev, (win - 1, lat, lon))

    tile = (slice(None), pl.ds(0, R), pl.ds(0, C))
    loads = [
        pltpu.make_async_copy(cells_h.at[0, 0], cells_v, load_sem.at[0]),
        pltpu.make_async_copy(ow_h.at[0, :, 0], ow_v, load_sem.at[1]),
        pltpu.make_async_copy(inc_h.at[0], x_ext.at[tile], load_sem.at[2]),
        pltpu.make_async_copy(winds_h.at[0], u_ext.at[tile], load_sem.at[3]),
        pltpu.make_async_copy(mw_h.at[0], mw_v, load_sem.at[4]),
        pltpu.make_async_copy(rea_h, rea_s, load_sem.at[5]),
    ]
    for load in loads:
        load.start()

    for d, (dlat, dlon) in enumerate(DIRS):
        for dw in range(2):
            there = lat_ok(-dlat) & (has_next if dw else (win >= 0))

            @pl.when(jnp.logical_not(there))
            def _(d=d, dw=dw, dlat=dlat, dlon=dlon):
                if dlon == 0:
                    ref = got_rows_far.at[d] if dw else got_rows_own.at[d]
                elif dlat == 0:
                    ref = got_cols.at[dw, d - 2]
                else:
                    ref = got_corner.at[dw, d - 4]
                ref[...] = jnp.zeros(ref.shape, F32)

    @pl.when(jnp.logical_not(has_next))
    def _():
        inc_n[...] = jnp.zeros(inc_n.shape, F32)
        mw_n[...] = jnp.zeros(mw_n.shape, F32)

    @pl.when(jnp.logical_not(has_prev))
    def _():
        got_fwd[...] = jnp.zeros(got_fwd.shape, F32)
        got_ring_r[...] = jnp.zeros(got_ring_r.shape, F32)
        got_ring_c[...] = jnp.zeros(got_ring_c.shape, F32)

    loads[0].wait()
    loads[1].wait()
    cells = cells_v[...]
    count = cells.shape[1]
    row_of = lax.shift_right_logical(cells, 8)
    col_of = lax.bitwise_and(cells, 255)
    at_row = iota((R, count), 0) == row_of
    at_col = jnp.where(iota((C, count), 0) == col_of, 1.0, 0.0).astype(BF16)
    for f in range(3):
        rest = ow_v[f]
        total = None
        for _ in range(3):
            part = rest.astype(BF16).astype(F32)
            rest = rest - part
            spread = jnp.where(at_row, part, 0.0).astype(BF16)
            term = lax.dot_general(spread, at_col, (((1,), (1,)), ((), ())), preferred_element_type=F32)
            total = term if total is None else total + term
        w_ext[f, 0:R, 0:C] = total

    for load in loads[2:]:
        load.wait()
    mix = [[rea_s[f, 0, g] + (KEEP if f == g else 0.0) for g in range(3)] for f in range(3)]

    lane = iota((R, 128), 1)
    packed = jnp.zeros((R, 128), F32)
    own = [(x_ext, 0), (x_ext, 1), (x_ext, 2), (u_ext, 0), (u_ext, 1), (w_ext, 0), (w_ext, 1), (w_ext, 2), (mw_v, 0), (mw_v, 1), (mw_v, 2)]
    for a, (ref, f) in enumerate(own):
        ends = jnp.where(lane < 64, ref[f, 0:R, 0:128], ref[f, 0:R, C - 128 : C])
        packed = jnp.where((lane >= 8 * a) & (lane < 8 * a + 8), rolled(ends, 8 * a + 4, 1), packed)
    pack[...] = packed
    half = R // 2
    low_lane = lax.rem(iota((half, 128), 1), 8) < 4
    ce[...] = jnp.where(low_lane, packed[:half], rolled(packed[half:], 4, 1))
    cw[...] = jnp.where(low_lane, rolled(packed[half:], -4, 1), packed[:half])

    sub = iota((8, C), 0)
    lu, lv = u_ext[0, R - 8 : R, 0:C], u_ext[1, R - 8 : R, 0:C]
    fu, fv = u_ext[0, 0:8, 0:C], u_ext[1, 0:8, 0:C]
    for f in range(3):
        wind = jnp.where(sub == 1, rolled(lv, -4 - f, 0), rolled(lu, -5 - f, 0))
        obs = rolled(w_ext[f, R - 8 : R, 0:C], 4, 0)
        rows_own[0, f] = jnp.where(sub >= 4, x_ext[f, R - 8 : R, 0:C], jnp.where(sub >= 2, obs, wind))
        wind = jnp.where(sub == 6, rolled(fu, 6 - f, 0), rolled(fv, 7 - f, 0))
        obs = rolled(w_ext[f, 0:8, 0:C], 4, 0)
        rows_own[1, f] = jnp.where(sub < 4, x_ext[f, 0:8, 0:C], jnp.where(sub < 6, obs, wind))
    for pair in range(2):
        n_rows = n_cols = None
        for f in range(2 * pair, min(3, 2 * pair + 2)):
            base = 4 * (f % 2)
            lx, lm = x_ext[f, R - 8 : R, 0:C], mw_v[f, R - 8 : R, 0:C]
            fx, fm = x_ext[f, 0:8, 0:C], mw_v[f, 0:8, 0:C]
            top = jnp.where(lax.rem(sub, 4) >= 2, rolled(lx, -base, 0), rolled(lm, -base - 2, 0))
            bottom = jnp.where(lax.rem(sub, 4) < 2, rolled(fx, base, 0), rolled(fm, base + 2, 0))
            n_rows = top if n_rows is None else jnp.where(sub < 4, top, n_rows)
            n_cols = bottom if n_cols is None else jnp.where(sub >= 4, bottom, n_cols)
        rows_far[0, pair] = n_rows
        rows_far[1, pair] = n_cols

    uc, vc = u_ext[0, 0:R, 0:C], u_ext[1, 0:R, 0:C]
    coef[0, 0:R, 0:C] = DIFFUSION - uc
    coef[1, 0:R, 0:C] = DIFFUSION + uc
    coef[2, 0:R, 0:C] = DIFFUSION - vc
    coef[3, 0:R, 0:C] = DIFFUSION + vc
    c_tile = [coef[i, 0:R, 0:C] for i in range(4)]
    state = [x_ext[f, 0:R, 0:C] for f in range(3)]
    for _ in range(2):
        state = tangent(state, c_tile, mix)
    for f in range(3):
        fwd0[f] = state[f]

    lats = 1 + lat_ok(1).astype(jnp.int32) + lat_ok(-1).astype(jnp.int32)
    prev, nxt = has_prev.astype(jnp.int32), has_next.astype(jnp.int32)
    pl.semaphore_wait(barrier, 3 * lats * (1 + prev) - 1 + nxt)

    def message(d, dw):
        dlat, dlon = DIRS[d]
        if dlon == 0:
            src, dst = (rows_far.at[d], got_rows_far.at[d]) if dw else (rows_own.at[d], got_rows_own.at[d])
        elif dlat == 0:
            src, dst = (ce if dlon == 1 else cw), got_cols.at[dw, d - 2]
        else:
            src, dst = pack.at[pl.ds(R - 8 if dlat == 1 else 0, 8)], got_corner.at[dw, d - 4]
        return pltpu.make_async_remote_copy(
            src_ref=src,
            dst_ref=dst,
            send_sem=send_sem.at[dw, d],
            recv_sem=recv_sem.at[dw, d],
            device_id=(win - dw, lat + dlat, lon_at(dlon)),
            device_id_type=MESH,
        )

    def across(i, src, dst, step):
        return pltpu.make_async_remote_copy(
            src_ref=src,
            dst_ref=dst,
            send_sem=xsend_sem.at[i],
            recv_sem=xrecv_sem.at[i],
            device_id=(win + step, lat, lon),
            device_id_type=MESH,
        )

    def copies(dw):
        for d, (dlat, _) in enumerate(DIRS):
            yield d, lat_ok(dlat) & (has_prev if dw else (win >= 0)), lat_ok(-dlat) & (has_next if dw else (win >= 0))

    for dw in range(2):
        for d, ok, _ in copies(dw):

            @pl.when(ok)
            def _(d=d, dw=dw):
                message(d, dw).start()

    bulk = [across(0, inc_h.at[0], inc_n, -1), across(1, mw_h.at[0], mw_n, -1)]
    first = across(2, fwd0, got_fwd, 1)
    late = [across(3, ring_r, got_ring_r, 1), across(4, ring_c, got_ring_c, 1)]

    @pl.when(has_next)
    def _():
        first.start()

    @pl.when(has_prev)
    def _():
        bulk[0].start()
        bulk[1].start()

    for dw in range(2):
        for d, _, ok in copies(dw):

            @pl.when(ok)
            def _(d=d, dw=dw):
                message(d, dw).wait_recv()

    corner_low = lax.rem(iota((8, 128), 1), 8) < 4
    corner_sub = iota((8, 128), 0)

    def columns(dw):
        from_west, from_east = got_cols[dw, 0], got_cols[dw, 1]
        upper = jnp.where(low_lane, from_west, from_east)
        lower = jnp.where(low_lane, rolled(from_west, -4, 1), rolled(from_east, 4, 1))
        sw, se, nw, ne = (got_corner[dw, i] for i in range(4))
        rim = jnp.where(corner_sub < 4, jnp.where(corner_low, nw, ne), jnp.where(corner_low, sw, se))
        return jnp.concatenate([upper, lower, rim], axis=0)

    own_cols = columns(0)

    def side(cols, a):
        return rolled(cols, -8 * a - 4, 1)

    E = R + 8
    inside = jnp.where(iota((8, C), 0) < 4, lat_ok(1).astype(F32), lat_ok(-1).astype(F32)) > 0.0
    for f in range(3):
        south_rows, north_rows = got_rows_own[0, f], got_rows_own[1, f]
        x_ext[f, :, C:] = side(own_cols, f)
        x_ext[f, R:E, 0:C] = jnp.where(sub < 4, north_rows, south_rows)
        w_ext[f, :, C:] = side(own_cols, 5 + f)
        w_ext[f, R:E, 0:C] = rolled(jnp.where(sub < 4, south_rows, north_rows), 4, 0)
    for i in range(2):
        rows = jnp.zeros((8, C), F32)
        for t in range(3):
            rows = jnp.where(sub == t, rolled(got_rows_own[1, t], t - 6 - i, 0), rows)
            rows = jnp.where(sub == 5 + t, rolled(got_rows_own[0, t], 5 + t - i, 0), rows)
        coef[2 * i, R:E, 0:C] = jnp.where(inside, DIFFUSION - rows, 0.0)
        coef[2 * i + 1, R:E, 0:C] = jnp.where(inside, DIFFUSION + rows, 0.0)
        cols = side(own_cols, 3 + i)
        less, more = DIFFUSION - cols, DIFFUSION + cols
        coef[2 * i, 0:R, C:] = less[0:R]
        coef[2 * i + 1, 0:R, C:] = more[0:R]
        coef[2 * i, R:E, C:] = jnp.where(inside[:, 0:128], less[R:E], 0.0)
        coef[2 * i + 1, R:E, C:] = jnp.where(inside[:, 0:128], more[R:E], 0.0)

    c_all = [coef[i] for i in range(4)]
    state = tangent([x_ext[f] for f in range(3)], c_all, mix)
    for f in range(3):
        t_ext[f] = state[f]
    state = tangent([t_ext[f] for f in range(3)], c_all, mix)

    ring = jnp.zeros((R, 128), F32)
    for f in range(3):
        t_ext[f] = state[f]
        ring_r[f] = jnp.where(sub < 4, t_ext[f, 0:8, 0:C], t_ext[f, R - 8 : R, 0:C])
        ends = jnp.where(lane < 64, t_ext[f, 0:R, 0:128], t_ext[f, 0:R, C - 128 : C])
        ring = jnp.where((lane >= 8 * f) & (lane < 8 * f + 8), rolled(ends, 8 * f + 4, 1), ring)
    quarter = R // 4
    folded = ring[0:quarter]
    group = iota((quarter, 128), 1)
    for q in range(1, 4):
        folded = jnp.where(group >= 32 * q, rolled(ring[quarter * q : quarter * (q + 1)], 32 * q, 1), folded)
    ring_c[...] = folded

    @pl.when(has_next)
    def _():
        late[0].start()
        late[1].start()

    far_cols = columns(1)

    @pl.when(has_next)
    def _():
        bulk[0].wait_recv()
        bulk[1].wait_recv()

    for f in range(3):
        t, base = f // 2, 4 * (f % 2)
        south_rows, north_rows = got_rows_far[0, t], got_rows_far[1, t]
        inc_rows = jnp.where(sub < 4, rolled(north_rows, -base, 0), rolled(south_rows, base, 0))
        mw_rows = jnp.where(sub < 4, rolled(north_rows, -base - 2, 0), rolled(south_rows, base + 2, 0))
        mw_cols = side(far_cols, 8 + f)
        g_ext[f, 0:R, 0:C] = w_ext[f, 0:R, 0:C] + mw_n[f]
        h_ext[f, 0:R, 0:C] = mw_n[f] * inc_n[f]
        g_ext[f, R:E, 0:C] = w_ext[f, R:E, 0:C] + mw_rows
        h_ext[f, R:E, 0:C] = mw_rows * inc_rows
        g_ext[f, :, C:] = w_ext[f, :, C:] + mw_cols
        h_ext[f, :, C:] = mw_cols * side(far_cols, f)

    state = [g_ext[f] * t_ext[f] - h_ext[f] for f in range(3)]
    state = adjoint(state, c_all, mix)
    for f in range(3):
        h_ext[f] = state[f]
    state = adjoint([h_ext[f] for f in range(3)], c_all, mix)
    for f in range(3):
        h_ext[f] = state[f]

    @pl.when(has_prev)
    def _():
        first.wait_recv()
        late[0].wait_recv()
        late[1].wait_recv()

    folded = got_ring_c[...]
    ring = jnp.concatenate([rolled(folded, -32 * q, 1) for q in range(4)], axis=0)
    for f in range(3):
        rows = got_ring_r[f]
        got_fwd[f, 0:8] = jnp.where(sub < 2, rows, got_fwd[f, 0:8])
        got_fwd[f, R - 8 : R] = jnp.where(sub >= 6, rows, got_fwd[f, R - 8 : R])
        cols = rolled(ring, -8 * f - 4, 1)
        got_fwd[f, :, 0:128] = jnp.where(lane < 2, cols, got_fwd[f, :, 0:128])
        got_fwd[f, :, C - 128 : C] = jnp.where(lane >= 126, cols, got_fwd[f, :, C - 128 : C])
        out_ref[0, f] = mw_v[f] * (x_ext[f, 0:R, 0:C] - got_fwd[f]) + h_ext[f, 0:R, 0:C]

    for dw in range(2):
        for d, ok, _ in copies(dw):

            @pl.when(ok)
            def _(d=d, dw=dw):
                message(d, dw).wait_send()

    @pl.when(has_next)
    def _():
        first.wait_send()
        late[0].wait_send()
        late[1].wait_send()

    @pl.when(has_prev)
    def _():
        bulk[0].wait_send()
        bulk[1].wait_send()


def per_device(sizes, *args):
    args = args[:3] + (jnp.transpose(args[3], (1, 0, 2)),) + args[4:]
    R, C = args[0].shape[-2:]
    count = args[4].shape[-1]
    ext = (R + 8, C + 128)
    vmem = lambda *shape: pltpu.VMEM(shape, F32)
    anywhere = pl.BlockSpec(memory_space=pl.ANY)
    return pl.pallas_call(
        functools.partial(kernel, sizes),
        out_shape=jax.ShapeDtypeStruct(args[0].shape, F32),
        in_specs=[anywhere] * 6,
        out_specs=pl.BlockSpec(memory_space=pltpu.VMEM),
        scratch_shapes=[
            vmem(3, *ext), vmem(2, *ext), vmem(3, *ext), vmem(4, *ext), vmem(3, *ext), vmem(3, *ext), vmem(3, *ext),
            vmem(3, R, C), pltpu.SMEM((3, 1, 3), F32), pltpu.VMEM((1, count), jnp.int32), vmem(3, 1, count),
            vmem(R, 128), vmem(R // 2, 128), vmem(R // 2, 128), vmem(2, 3, 8, C), vmem(2, 2, 8, C),
            vmem(3, R, C), vmem(3, 8, C), vmem(R // 4, 128),
            vmem(2, 3, 8, C), vmem(2, 2, 8, C), vmem(2, 2, R // 2, 128), vmem(2, 4, 8, 128),
            vmem(3, R, C), vmem(3, R, C), vmem(3, R, C), vmem(3, 8, C), vmem(R // 4, 128),
            pltpu.SemaphoreType.DMA((6,)), pltpu.SemaphoreType.DMA((2, 8)), pltpu.SemaphoreType.DMA((2, 8)),
            pltpu.SemaphoreType.DMA((5,)), pltpu.SemaphoreType.DMA((5,)),
        ],
        compiler_params=pltpu.CompilerParams(
            collective_id=0, has_side_effects=True, vmem_limit_bytes=60 * 1024 * 1024
        ),
        cost_estimate=pl.CostEstimate(flops=10_000_000, bytes_accessed=1_000_000, transcendentals=0),
        name="window_product",
    )(*args)


def solution(mesh):
    sizes = tuple(mesh.shape[name] for name in ("win", "lat", "lon"))
    in_specs = (
        P("win", None, "lat", "lon"),
        P("win", None, "lat", "lon"),
        P("win", None, "lat", "lon"),
        P("win", None, None),
        P("win", "lat", "lon", None),
        P("win", None, "lat", "lon", None),
    )
    out_specs = P("win", None, "lat", "lon")
    return jax.shard_map(
        functools.partial(per_device, sizes), mesh=mesh, in_specs=in_specs, out_specs=out_specs, check_vma=False
    )
```

```python
import functools

import jax
import jax.numpy as jnp
from jax import lax
from jax.experimental import pallas as pl
from jax.experimental.pallas import tpu as pltpu
from jax.sharding import PartitionSpec as P

DIFFUSION = 0.15
KEEP = 1.0 - 4.0 * DIFFUSION
MESH = pl.DeviceIdType.MESH
F32 = jnp.float32
BF16 = jnp.bfloat16
DIRS = ((1, 0), (-1, 0), (0, 1), (0, -1), (1, 1), (1, -1), (-1, 1), (-1, -1))


def rolled(x, shift, axis):
    shift = shift % x.shape[axis]
    return x if shift == 0 else pltpu.roll(x, shift, axis)


def east(x):
    return rolled(x, -1, 1)


def west(x):
    return rolled(x, 1, 1)


def north(x):
    return rolled(x, -1, 0)


def south(x):
    return rolled(x, 1, 0)


def tangent(xs, coef, mix):
    a, b, c, d = coef
    out = []
    for f in range(3):
        x = xs[f]
        y = a * east(x) + b * west(x) + c * north(x) + d * south(x)
        out.append(y + mix[f][0] * xs[0] + mix[f][1] * xs[1] + mix[f][2] * xs[2])
    return out


def adjoint(zs, coef, mix):
    a, b, c, d = coef
    out = []
    for f in range(3):
        z = zs[f]
        y = east(b * z) + west(a * z) + north(d * z) + south(c * z)
        out.append(y + mix[0][f] * zs[0] + mix[1][f] * zs[1] + mix[2][f] * zs[2])
    return out


def iota(shape, axis):
    return lax.broadcasted_iota(jnp.int32, shape, axis)


def kernel(
    sizes,
    inc_h, mw_h, winds_h, rea_h, cells_h, ow_h,
    out_ref,
    x_ext, u_ext, w_ext, coef, g_ext, h_ext, t_ext,
    mw_v, rea_s, cells_v, ow_v,
    pack, cols, rows_own, rows_far, fwd0, ring_r, ring_c,
    got_rows_own, got_rows_far, got_cols, got_corner, inc_n, mw_n, got_fwd, got_ring_r, got_ring_c,
    load_sem, send_sem, recv_sem, xsend_sem, xrecv_sem, gate, far_ok,
):
    n_win, n_lat, n_lon = sizes
    win, lat, lon = lax.axis_index("win"), lax.axis_index("lat"), lax.axis_index("lon")
    R, C = 64, 256

    def lon_at(step):
        return lax.rem(lon + step + n_lon, n_lon)

    def lat_ok(step):
        return (lat + step >= 0) & (lat + step < n_lat)

    has_prev, has_next = win > 0, win < n_win - 1
    mid = n_lat // 2

    def is_last(at_lat, at_lon):
        return (at_lat == mid - 1) & (at_lon == n_lon - 1)

    def is_first(at_lat, at_lon):
        return (at_lat == mid) & (at_lon == 0)

    def meets_origin(at_win, at_lat, at_lon):
        return (at_win < 2) & (at_lat < 2) & (at_lon == n_lon - 1)

    def deferred(at_win, at_lat, at_lon, d, dw):
        dlat, dlon = DIRS[d]
        held = lat < 0
        if dlat == 1 and dlon <= 0:
            held = held | is_last(at_lat, at_lon)
        if dlon == -1 and dlat >= 0:
            held = held | is_first(at_lat, at_lon)
        if dlon == 1 and dlat <= 0:
            held = held | ((at_win == dw) & (at_lat == -dlat) & (at_lon == n_lon - 1))
        return held

    def answered(at_win, at_lat, at_lon, d):
        dlat, dlon = DIRS[d]
        early = lat < 0
        if dlon == -1:
            early = early | ((at_lon == 0) & (at_lat < mid) & (at_lat + dlat < mid))
        if dlat == 1:
            early = early | ((at_lat == mid - 1) & (at_lon < n_lon // 2))
        return early & ((at_win > 0) | (at_lat > 0) | (at_lon > 0))

    def turn(d):
        dlat, dlon = DIRS[d]
        urgent = later = lat < 0
        if dlat == -1:
            urgent = urgent | (lat == mid)
        if dlon == 1:
            urgent = urgent | (lon == n_lon - 1)
        if dlat == 1:
            later = later | (lat == mid - 1)
        if dlon == -1:
            later = later | (lon == 0)
        return jnp.where(urgent, 0, jnp.where(later, 2, 1))

    tile = (slice(None), pl.ds(0, R), pl.ds(0, C))
    loads = [
        pltpu.make_async_copy(cells_h.at[0, 0], cells_v, load_sem.at[0]),
        pltpu.make_async_copy(ow_h.at[0, :, 0], ow_v, load_sem.at[1]),
        pltpu.make_async_copy(inc_h.at[0], x_ext.at[tile], load_sem.at[2]),
        pltpu.make_async_copy(winds_h.at[0], u_ext.at[tile], load_sem.at[3]),
        pltpu.make_async_copy(mw_h.at[0], mw_v, load_sem.at[4]),
        pltpu.make_async_copy(rea_h, rea_s, load_sem.at[5]),
    ]
    for load in loads:
        load.start()

    barrier = pltpu.get_barrier_semaphore()

    def tell(ok, target):
        @pl.when(ok)
        def _():
            pl.semaphore_signal(barrier, inc=1, device_id=target, device_id_type=MESH)

    for d, (dlat, dlon) in enumerate(DIRS):
        for dw in range(2):
            source = (win + dw, lat - dlat, lon_at(-dlon))
            ok = lat_ok(-dlat) & jnp.logical_not(deferred(*source, d, dw) | answered(*source, d))
            tell(ok & has_next if dw else ok, source)
        tell(has_prev & lat_ok(dlat) & answered(win, lat, lon, d), (win - 1, lat + dlat, lon_at(dlon)))
    origin = (win == 0) & (lat == 0) & (lon == 0)
    tell(origin, (win, lat, lon_at(-2)))
    tell(origin & has_next, (win + 1, lat, lon_at(-2)))
    tell(has_next, (win + 1, lat, lon))
    tell(has_prev, (win - 1, lat, lon))

    for d, (dlat, dlon) in enumerate(DIRS):
        for dw in range(2):
            there = lat_ok(-dlat) & (has_next if dw else (win >= 0))

            @pl.when(jnp.logical_not(there))
            def _(d=d, dw=dw, dlat=dlat, dlon=dlon):
                if dlon == 0:
                    ref = got_rows_far.at[d] if dw else got_rows_own.at[d]
                elif dlat == 0:
                    ref = got_cols.at[dw, d - 2]
                else:
                    ref = got_corner.at[dw, d - 4]
                ref[...] = jnp.zeros(ref.shape, F32)

    @pl.when(jnp.logical_not(has_next))
    def _():
        inc_n[...] = jnp.zeros(inc_n.shape, F32)
        mw_n[...] = jnp.zeros(mw_n.shape, F32)

    @pl.when(jnp.logical_not(has_prev))
    def _():
        got_fwd[...] = jnp.zeros(got_fwd.shape, F32)
        got_ring_r[...] = jnp.zeros(got_ring_r.shape, F32)
        got_ring_c[...] = jnp.zeros(got_ring_c.shape, F32)

    loads[0].wait()
    loads[1].wait()
    cells = cells_v[...]
    count = cells.shape[1]
    row_of = lax.shift_right_logical(cells, 8)
    col_of = lax.bitwise_and(cells, 255)
    at_row = iota((R, count), 0) == row_of
    at_col = jnp.where(iota((C, count), 0) == col_of, 1.0, 0.0).astype(BF16)
    for f in range(3):
        rest = ow_v[f]
        total = None
        for _ in range(3):
            part = rest.astype(BF16).astype(F32)
            rest = rest - part
            spread = jnp.where(at_row, part, 0.0).astype(BF16)
            term = lax.dot_general(spread, at_col, (((1,), (1,)), ((), ())), preferred_element_type=F32)
            total = term if total is None else total + term
        w_ext[f, 0:R, 0:C] = total

    for load in loads[2:]:
        load.wait()
    mix = [[rea_s[f, 0, g] + (KEEP if f == g else 0.0) for g in range(3)] for f in range(3)]

    lane = iota((R, 128), 1)
    packed = jnp.zeros((R, 128), F32)
    own = [(x_ext, 0), (x_ext, 1), (x_ext, 2), (u_ext, 0), (u_ext, 1), (w_ext, 0), (w_ext, 1), (w_ext, 2), (mw_v, 0), (mw_v, 1), (mw_v, 2), (x_ext, 0), (x_ext, 1), (x_ext, 2)]
    for a, (ref, f) in enumerate(own):
        ends = jnp.where(lane < 64, ref[f, 0:R, 0:128], ref[f, 0:R, C - 128 : C])
        packed = jnp.where((lane >= 8 * a) & (lane < 8 * a + 8), rolled(ends, 8 * a + 4, 1), packed)
    pack[...] = packed
    half = R // 2
    low_lane = lax.rem(iota((half, 128), 1), 8) < 4
    left = iota((half // 2, 128), 1) < 64
    for e, pair in enumerate((
        jnp.where(low_lane, packed[:half], rolled(packed[half:], 4, 1)),
        jnp.where(low_lane, rolled(packed[half:], -4, 1), packed[:half]),
    )):
        upper, lower = pair[: half // 2], pair[half // 2 :]
        cols[0, e] = jnp.where(left, upper, rolled(lower, 64, 1))
        cols[1, e] = jnp.where(left, rolled(upper, 64, 1), lower)

    sub = iota((8, C), 0)
    lu, lv = u_ext[0, R - 8 : R, 0:C], u_ext[1, R - 8 : R, 0:C]
    fu, fv = u_ext[0, 0:8, 0:C], u_ext[1, 0:8, 0:C]
    for f in range(3):
        wind = jnp.where(sub == 1, rolled(lv, -4 - f, 0), rolled(lu, -5 - f, 0))
        obs = rolled(w_ext[f, R - 8 : R, 0:C], 4, 0)
        rows_own[0, f] = jnp.where(sub >= 4, x_ext[f, R - 8 : R, 0:C], jnp.where(sub >= 2, obs, wind))
        wind = jnp.where(sub == 6, rolled(fu, 6 - f, 0), rolled(fv, 7 - f, 0))
        obs = rolled(w_ext[f, 0:8, 0:C], 4, 0)
        rows_own[1, f] = jnp.where(sub < 4, x_ext[f, 0:8, 0:C], jnp.where(sub < 6, obs, wind))
    for pair in range(2):
        n_rows = n_cols = None
        for f in range(2 * pair, min(3, 2 * pair + 2)):
            base = 4 * (f % 2)
            lx, lm = x_ext[f, R - 8 : R, 0:C], mw_v[f, R - 8 : R, 0:C]
            fx, fm = x_ext[f, 0:8, 0:C], mw_v[f, 0:8, 0:C]
            top = jnp.where(lax.rem(sub, 4) >= 2, rolled(lx, -base, 0), rolled(lm, -base - 2, 0))
            bottom = jnp.where(lax.rem(sub, 4) < 2, rolled(fx, base, 0), rolled(fm, base + 2, 0))
            n_rows = top if n_rows is None else jnp.where(sub < 4, top, n_rows)
            n_cols = bottom if n_cols is None else jnp.where(sub >= 4, bottom, n_cols)
        rows_far[0, pair] = n_rows
        rows_far[1, pair] = n_cols

    lats = 1 + lat_ok(1).astype(jnp.int32) + lat_ok(-1).astype(jnp.int32)
    prev, nxt = has_prev.astype(jnp.int32), has_next.astype(jnp.int32)
    ends = (is_last(lat, lon) | is_first(lat, lon)).astype(jnp.int32)
    meets = meets_origin(win, lat, lon).astype(jnp.int32)
    knows_origin = (win < 2) & (lat == 0) & (lon == n_lon - 2)
    asks = owed = jnp.int32(0)
    for d, (dlat, dlon) in enumerate(DIRS):
        asks += (lat_ok(dlat) & answered(win, lat, lon, d)).astype(jnp.int32)
        owed += (lat_ok(-dlat) & answered(win + 1, lat - dlat, lon_at(-dlon), d)).astype(jnp.int32)
    others = (3 * lats - 2 * ends - asks) * (1 + prev) - 1 + nxt + owed * nxt
    pl.semaphore_wait(barrier, others - meets + knows_origin.astype(jnp.int32))

    def message(d, dw):
        dlat, dlon = DIRS[d]
        if dlon == 0:
            src, dst = (rows_far.at[d], got_rows_far.at[d]) if dw else (rows_own.at[d], got_rows_own.at[d])
        elif dlat == 0:
            src, dst = cols.at[dw, d - 2], got_cols.at[dw, d - 2]
        else:
            src, dst = pack.at[pl.ds(R - 8 if dlat == 1 else 0, 8)], got_corner.at[dw, d - 4]
        return pltpu.make_async_remote_copy(
            src_ref=src,
            dst_ref=dst,
            send_sem=send_sem.at[dw, d],
            recv_sem=recv_sem.at[dw, d],
            device_id=(win - dw, lat + dlat, lon_at(dlon)),
            device_id_type=MESH,
        )

    def across(i, src, dst, step):
        return pltpu.make_async_remote_copy(
            src_ref=src,
            dst_ref=dst,
            send_sem=xsend_sem.at[i],
            recv_sem=xrecv_sem.at[i],
            device_id=(win + step, lat, lon),
            device_id_type=MESH,
        )

    def copies(dw):
        for d, (dlat, _) in enumerate(DIRS):
            yield d, lat_ok(dlat) & (has_prev if dw else (win >= 0)), lat_ok(-dlat) & (has_next if dw else (win >= 0))

    def answer():
        for dw in range(2):
            for d, _, ok in copies(dw):
                dlat, dlon = DIRS[d]
                source = (win + dw, lat - dlat, lon_at(-dlon))

                @pl.when(ok & answered(*source, d))
                def _(source=source):
                    pl.semaphore_signal(far_ok, inc=1, device_id=source, device_id_type=MESH)

    for now in range(3):
        for dw in range(2):
            for d, ok, _ in copies(dw):

                @pl.when(ok & (turn(d) == now) & jnp.logical_not(deferred(win, lat, lon, d, dw) | answered(win, lat, lon, d)))
                def _(d=d, dw=dw):
                    message(d, dw).start()

        if now == 0:
            answer()

    bulk = [across(0, inc_h.at[0], inc_n, -1), across(1, mw_h.at[0], mw_n, -1)]
    first = across(2, fwd0, got_fwd, 1)
    late = [across(3, ring_r, got_ring_r, 1), across(4, ring_c, got_ring_c, 1)]

    @pl.when(has_prev)
    def _():
        bulk[0].start()
        bulk[1].start()

    @pl.when((lat == mid - 1) & (lon == n_lon - 2))
    def _():
        pl.semaphore_signal(gate, inc=1, device_id=(win, lat, lon + 1), device_id_type=MESH)

    @pl.when(knows_origin)
    def _():
        pl.semaphore_signal(gate, inc=1, device_id=(win, lat, lon + 1), device_id_type=MESH)
        pl.semaphore_signal(gate, inc=1, device_id=(win, lat + 1, lon + 1), device_id_type=MESH)

    @pl.when((lat == mid + 1) & (lon == 0))
    def _():
        pl.semaphore_signal(gate, inc=1, device_id=(win, lat - 1, lon), device_id_type=MESH)

    uc, vc = u_ext[0, 0:R, 0:C], u_ext[1, 0:R, 0:C]
    coef[0, 0:R, 0:C] = DIFFUSION - uc
    coef[1, 0:R, 0:C] = DIFFUSION + uc
    coef[2, 0:R, 0:C] = DIFFUSION - vc
    coef[3, 0:R, 0:C] = DIFFUSION + vc
    c_tile = [coef[i, 0:R, 0:C] for i in range(4)]
    state = [x_ext[f, 0:R, 0:C] for f in range(3)]
    for _ in range(2):
        state = tangent(state, c_tile, mix)
    for f in range(3):
        fwd0[f] = state[f]

    @pl.when(has_next)
    def _():
        first.start()

    @pl.when(ends + meets > 0)
    def _():
        pl.semaphore_wait(gate, ends + meets)
        for dw in range(2):
            for d, ok, _ in copies(dw):

                @pl.when(ok & deferred(win, lat, lon, d, dw))
                def _(d=d, dw=dw):
                    message(d, dw).start()

    @pl.when(asks > 0)
    def _():
        pl.semaphore_wait(far_ok, asks * (1 + prev))
        for dw in range(2):
            for d, ok, _ in copies(dw):

                @pl.when(ok & answered(win, lat, lon, d))
                def _(d=d, dw=dw):
                    message(d, dw).start()

    def arrive(dw):
        for d, _, ok in copies(dw):

            @pl.when(ok)
            def _(d=d, dw=dw):
                message(d, dw).wait_recv()

    arrive(0)

    corner_low = lax.rem(iota((8, 128), 1), 8) < 4
    corner_sub = iota((8, 128), 0)

    def columns(dw):
        from_west, from_east = (
            jnp.concatenate([got_cols[dw, i], rolled(got_cols[dw, i], 64, 1)], axis=0) for i in range(2)
        )
        upper = jnp.where(low_lane, from_west, from_east)
        lower = jnp.where(low_lane, rolled(from_west, -4, 1), rolled(from_east, 4, 1))
        sw, se, nw, ne = (got_corner[dw, i] for i in range(4))
        rim = jnp.where(corner_sub < 4, jnp.where(corner_low, nw, ne), jnp.where(corner_low, sw, se))
        return jnp.concatenate([upper, lower, rolled(rim, 64, 1) if dw else rim], axis=0)

    own_cols = columns(0)

    def side(ends, a):
        return rolled(ends, -8 * a - 4, 1)

    E = R + 8
    inside = jnp.where(iota((8, C), 0) < 4, lat_ok(1).astype(F32), lat_ok(-1).astype(F32)) > 0.0
    for f in range(3):
        south_rows, north_rows = got_rows_own[0, f], got_rows_own[1, f]
        x_ext[f, :, C:] = side(own_cols, f)
        x_ext[f, R:E, 0:C] = jnp.where(sub < 4, north_rows, south_rows)
        w_ext[f, :, C:] = side(own_cols, 5 + f)
        w_ext[f, R:E, 0:C] = rolled(jnp.where(sub < 4, south_rows, north_rows), 4, 0)
    for i in range(2):
        rows = jnp.zeros((8, C), F32)
        for t in range(3):
            rows = jnp.where(sub == t, rolled(got_rows_own[1, t], t - 6 - i, 0), rows)
            rows = jnp.where(sub == 5 + t, rolled(got_rows_own[0, t], 5 + t - i, 0), rows)
        coef[2 * i, R:E, 0:C] = jnp.where(inside, DIFFUSION - rows, 0.0)
        coef[2 * i + 1, R:E, 0:C] = jnp.where(inside, DIFFUSION + rows, 0.0)
        ends = side(own_cols, 3 + i)
        less, more = DIFFUSION - ends, DIFFUSION + ends
        coef[2 * i, 0:R, C:] = less[0:R]
        coef[2 * i + 1, 0:R, C:] = more[0:R]
        coef[2 * i, R:E, C:] = jnp.where(inside[:, 0:128], less[R:E], 0.0)
        coef[2 * i + 1, R:E, C:] = jnp.where(inside[:, 0:128], more[R:E], 0.0)

    c_all = [coef[i] for i in range(4)]
    state = tangent([x_ext[f] for f in range(3)], c_all, mix)
    for f in range(3):
        t_ext[f] = state[f]
    state = tangent([t_ext[f] for f in range(3)], c_all, mix)

    ring = jnp.zeros((R, 128), F32)
    for f in range(3):
        t_ext[f] = state[f]
        ring_r[f] = jnp.where(sub < 4, t_ext[f, 0:8, 0:C], t_ext[f, R - 8 : R, 0:C])
        ends = jnp.where(lane < 64, t_ext[f, 0:R, 0:128], t_ext[f, 0:R, C - 128 : C])
        ring = jnp.where((lane >= 8 * f) & (lane < 8 * f + 8), rolled(ends, 8 * f + 4, 1), ring)
    quarter = R // 4
    folded = ring[0:quarter]
    group = iota((quarter, 128), 1)
    for q in range(1, 4):
        folded = jnp.where(group >= 32 * q, rolled(ring[quarter * q : quarter * (q + 1)], 32 * q, 1), folded)
    ring_c[...] = folded

    @pl.when(has_next)
    def _():
        late[0].start()
        late[1].start()

    arrive(1)
    far_cols = columns(1)

    @pl.when(has_next)
    def _():
        bulk[0].wait_recv()
        bulk[1].wait_recv()

    for f in range(3):
        t, base = f // 2, 4 * (f % 2)
        south_rows, north_rows = got_rows_far[0, t], got_rows_far[1, t]
        inc_rows = jnp.where(sub < 4, rolled(north_rows, -base, 0), rolled(south_rows, base, 0))
        mw_rows = jnp.where(sub < 4, rolled(north_rows, -base - 2, 0), rolled(south_rows, base + 2, 0))
        mw_cols = side(far_cols, f)
        g_ext[f, 0:R, 0:C] = w_ext[f, 0:R, 0:C] + mw_n[f]
        h_ext[f, 0:R, 0:C] = mw_n[f] * inc_n[f]
        g_ext[f, R:E, 0:C] = w_ext[f, R:E, 0:C] + mw_rows
        h_ext[f, R:E, 0:C] = mw_rows * inc_rows
        g_ext[f, :, C:] = w_ext[f, :, C:] + mw_cols
        h_ext[f, :, C:] = mw_cols * side(far_cols, 3 + f)

    state = [g_ext[f] * t_ext[f] - h_ext[f] for f in range(3)]
    state = adjoint(state, c_all, mix)
    for f in range(3):
        h_ext[f] = state[f]
    state = adjoint([h_ext[f] for f in range(3)], c_all, mix)
    for f in range(3):
        h_ext[f] = state[f]

    @pl.when(has_prev)
    def _():
        first.wait_recv()
        late[0].wait_recv()
        late[1].wait_recv()

    folded = got_ring_c[...]
    ring = jnp.concatenate([rolled(folded, -32 * q, 1) for q in range(4)], axis=0)
    for f in range(3):
        rows = got_ring_r[f]
        got_fwd[f, 0:8] = jnp.where(sub < 2, rows, got_fwd[f, 0:8])
        got_fwd[f, R - 8 : R] = jnp.where(sub >= 6, rows, got_fwd[f, R - 8 : R])
        ends = rolled(ring, -8 * f - 4, 1)
        got_fwd[f, :, 0:128] = jnp.where(lane < 2, ends, got_fwd[f, :, 0:128])
        got_fwd[f, :, C - 128 : C] = jnp.where(lane >= 126, ends, got_fwd[f, :, C - 128 : C])
        out_ref[0, f] = mw_v[f] * (x_ext[f, 0:R, 0:C] - got_fwd[f]) + h_ext[f, 0:R, 0:C]

    for dw in range(2):
        for d, ok, _ in copies(dw):

            @pl.when(ok)
            def _(d=d, dw=dw):
                message(d, dw).wait_send()

    @pl.when(has_next)
    def _():
        first.wait_send()
        late[0].wait_send()
        late[1].wait_send()

    @pl.when(has_prev)
    def _():
        bulk[0].wait_send()
        bulk[1].wait_send()


def per_device(sizes, *args):
    args = args[:3] + (jnp.transpose(args[3], (1, 0, 2)),) + args[4:]
    R, C = args[0].shape[-2:]
    count = args[4].shape[-1]
    args = [pltpu.with_memory_space_constraint(a, pltpu.HBM) for a in args]
    ext = (R + 8, C + 128)
    vmem = lambda *shape: pltpu.VMEM(shape, F32)
    anywhere = pl.BlockSpec(memory_space=pl.ANY)
    return pl.pallas_call(
        functools.partial(kernel, sizes),
        out_shape=jax.ShapeDtypeStruct(args[0].shape, F32),
        in_specs=[anywhere] * 6,
        out_specs=pl.BlockSpec(memory_space=pltpu.VMEM),
        scratch_shapes=[
            vmem(3, *ext), vmem(2, *ext), vmem(3, *ext), vmem(4, *ext), vmem(3, *ext), vmem(3, *ext), vmem(3, *ext),
            vmem(3, R, C), pltpu.SMEM((3, 1, 3), F32), pltpu.VMEM((1, count), jnp.int32), vmem(3, 1, count),
            vmem(R, 128), vmem(2, 2, R // 4, 128), vmem(2, 3, 8, C), vmem(2, 2, 8, C),
            vmem(3, R, C), vmem(3, 8, C), vmem(R // 4, 128),
            vmem(2, 3, 8, C), vmem(2, 2, 8, C), vmem(2, 2, R // 4, 128), vmem(2, 4, 8, 128),
            vmem(3, R, C), vmem(3, R, C), vmem(3, R, C), vmem(3, 8, C), vmem(R // 4, 128),
            pltpu.SemaphoreType.DMA((6,)), pltpu.SemaphoreType.DMA((2, 8)), pltpu.SemaphoreType.DMA((2, 8)),
            pltpu.SemaphoreType.DMA((5,)), pltpu.SemaphoreType.DMA((5,)), pltpu.SemaphoreType.REGULAR,
            pltpu.SemaphoreType.REGULAR,
        ],
        compiler_params=pltpu.CompilerParams(
            collective_id=0, has_side_effects=True, vmem_limit_bytes=32 * 1024 * 1024
        ),
        cost_estimate=pl.CostEstimate(flops=10_000_000, bytes_accessed=1_000_000, transcendentals=0),
        name="window_product",
    )(*args)


def solution(mesh):
    sizes = tuple(mesh.shape[name] for name in ("win", "lat", "lon"))
    in_specs = (
        P("win", None, "lat", "lon"),
        P("win", None, "lat", "lon"),
        P("win", None, "lat", "lon"),
        P("win", None, None),
        P("win", "lat", "lon", None),
        P("win", None, "lat", "lon", None),
    )
    out_specs = P("win", None, "lat", "lon")
    return jax.shard_map(
        functools.partial(per_device, sizes), mesh=mesh, in_specs=in_specs, out_specs=out_specs, check_vma=False
    )
```

```python
import functools

import jax
import jax.numpy as jnp
from jax import lax
from jax.experimental import pallas as pl
from jax.experimental.pallas import tpu as pltpu
from jax.sharding import PartitionSpec as P

DIFFUSION = 0.15
KEEP = 1.0 - 4.0 * DIFFUSION
MESH = pl.DeviceIdType.MESH
F32 = jnp.float32
BF16 = jnp.bfloat16
DIRS = ((1, 0), (-1, 0), (0, 1), (0, -1), (1, 1), (1, -1), (-1, 1), (-1, -1))


def rolled(x, shift, axis):
    shift = shift % x.shape[axis]
    return x if shift == 0 else pltpu.roll(x, shift, axis)


def east(x):
    return rolled(x, -1, 1)


def west(x):
    return rolled(x, 1, 1)


def north(x):
    return rolled(x, -1, 0)


def south(x):
    return rolled(x, 1, 0)


def tangent(xs, coef, mix):
    a, b, c, d = coef
    out = []
    for f in range(3):
        x = xs[f]
        y = a * east(x) + b * west(x) + c * north(x) + d * south(x)
        out.append(y + mix[f][0] * xs[0] + mix[f][1] * xs[1] + mix[f][2] * xs[2])
    return out


def adjoint(zs, coef, mix):
    a, b, c, d = coef
    out = []
    for f in range(3):
        z = zs[f]
        y = east(b * z) + west(a * z) + north(d * z) + south(c * z)
        out.append(y + mix[0][f] * zs[0] + mix[1][f] * zs[1] + mix[2][f] * zs[2])
    return out


def iota(shape, axis):
    return lax.broadcasted_iota(jnp.int32, shape, axis)


def kernel(
    sizes,
    inc_h, mw_h, winds_h, rea_h, cells_h, ow_h,
    out_ref,
    x_ext, u_ext, w_ext, coef, g_ext, h_ext, t_ext,
    mw_v, rea_s, cells_v, ow_v,
    pack, cols, rows_own, rows_far, fwd0, ring_r, ring_c,
    got_rows_own, got_rows_far, got_cols, got_corner, inc_n, mw_n, got_fwd, got_ring_r, got_ring_c,
    load_sem, send_sem, recv_sem, xsend_sem, xrecv_sem, fsend_sem, frecv_sem, gate, far_ok,
    prev_rows, prev_cols, prev_corner, prev_inc, prev_wind, prev_rea, prev_rea_s, xp_ext, cp_ext,
):
    n_win, n_lat, n_lon = sizes
    win, lat, lon = lax.axis_index("win"), lax.axis_index("lat"), lax.axis_index("lon")
    R, C = 64, 256

    def lon_at(step):
        return lax.rem(lon + step + n_lon, n_lon)

    def lat_ok(step):
        return (lat + step >= 0) & (lat + step < n_lat)

    has_prev, has_next = win > 0, win < n_win - 1
    mid = n_lat // 2

    def is_last(at_lat, at_lon):
        return (at_lat == mid - 1) & (at_lon == n_lon - 1)

    def is_first(at_lat, at_lon):
        return (at_lat == mid) & (at_lon == 0)

    def is_corner(at_lat, at_lon):
        return (at_lat == mid) & (at_lon == n_lon - 1)

    def meets_origin(at_win, at_lat, at_lon):
        return (at_win < 2) & (at_lat < 2) & (at_lon == n_lon - 1)

    def deferred(at_win, at_lat, at_lon, d, dw):
        dlat, dlon = DIRS[d]
        held = lat < 0
        if dlat == 1 and dlon <= 0:
            held = held | is_last(at_lat, at_lon)
        if dlon == -1 and dlat >= 0:
            held = held | is_first(at_lat, at_lon)
        if (dlat == -1 and dlon <= 0) or (dlon == 1 and dlat >= 0):
            held = held | is_corner(at_lat, at_lon)
        if dlon == 1 and dlat <= 0:
            held = held | ((at_win == dw) & (at_lat == -dlat) & (at_lon == n_lon - 1))
        return held

    def answered(at_win, at_lat, at_lon, d):
        dlat, dlon = DIRS[d]
        early = lat < 0
        if dlon == -1:
            early = early | ((at_lon == 0) & (at_lat < mid) & (at_lat + dlat < mid))
        if dlat == 1:
            early = early | ((at_lat == mid - 1) & (at_lon < n_lon // 2))
        return early & ((at_win > 0) | (at_lat > 0) | (at_lon > 0))

    def turn(d):
        dlat, dlon = DIRS[d]
        urgent = later = lat < 0
        if dlat == -1:
            urgent = urgent | (lat == mid)
        if dlon == 1:
            urgent = urgent | (lon == n_lon - 1)
        if dlat == 1:
            later = later | (lat == mid - 1)
        if dlon == -1:
            later = later | (lon == 0)
        return jnp.where(urgent, 0, jnp.where(later, 2, 1))

    tile = (slice(None), pl.ds(0, R), pl.ds(0, C))
    loads = [
        pltpu.make_async_copy(cells_h.at[0, 0], cells_v, load_sem.at[0]),
        pltpu.make_async_copy(ow_h.at[0, :, 0], ow_v, load_sem.at[1]),
        pltpu.make_async_copy(inc_h.at[0], x_ext.at[tile], load_sem.at[2]),
        pltpu.make_async_copy(winds_h.at[0], u_ext.at[tile], load_sem.at[3]),
        pltpu.make_async_copy(mw_h.at[0], mw_v, load_sem.at[4]),
        pltpu.make_async_copy(rea_h, rea_s, load_sem.at[5]),
    ]
    for load in loads:
        load.start()

    barrier = pltpu.get_barrier_semaphore()

    def tell(ok, target):
        @pl.when(ok)
        def _():
            pl.semaphore_signal(barrier, inc=1, device_id=target, device_id_type=MESH)

    for d, (dlat, dlon) in enumerate(DIRS):
        for dw in range(2):
            source = (win + dw, lat - dlat, lon_at(-dlon))
            ok = lat_ok(-dlat) & jnp.logical_not(deferred(*source, d, dw) | answered(*source, d))
            tell(ok & has_next if dw else ok, source)
        tell(has_prev & lat_ok(dlat) & answered(win, lat, lon, d), (win - 1, lat + dlat, lon_at(dlon)))
    origin = (win == 0) & (lat == 0) & (lon == 0)
    follower = (win == 1) & (lat == 0) & (lon == 0)
    feeds = {
        d: has_next & (win == 0) & (lat == -dlat) & (lon_at(dlon) == 0)
        for d, (dlat, dlon) in enumerate(DIRS)
        if dlat <= 0
    }
    for d in feeds:
        tell(follower, (win - 1, lat - DIRS[d][0], lon_at(-DIRS[d][1])))
    tell(origin, (win, lat, lon_at(-2)))
    tell(origin & has_next, (win + 1, lat, lon_at(-2)))
    tell(has_next, (win + 1, lat, lon))
    tell(has_prev, (win - 1, lat, lon))

    for d, (dlat, dlon) in enumerate(DIRS):
        for dw in range(2):
            there = lat_ok(-dlat) & (has_next if dw else (win >= 0))

            @pl.when(jnp.logical_not(there))
            def _(d=d, dw=dw, dlat=dlat, dlon=dlon):
                if dlon == 0:
                    ref = got_rows_far.at[d] if dw else got_rows_own.at[d]
                elif dlat == 0:
                    ref = got_cols.at[dw, d - 2]
                else:
                    ref = got_corner.at[dw, d - 4]
                ref[...] = jnp.zeros(ref.shape, F32)

    @pl.when(follower)
    def _():
        prev_rows[0] = jnp.zeros(prev_rows.shape[1:], F32)
        for i, (dlat, _) in enumerate(DIRS[4:]):
            if dlat > 0:
                prev_corner[i] = jnp.zeros(prev_corner.shape[1:], F32)

    @pl.when(jnp.logical_not(has_next))
    def _():
        inc_n[...] = jnp.zeros(inc_n.shape, F32)
        mw_n[...] = jnp.zeros(mw_n.shape, F32)

    @pl.when(jnp.logical_not(has_prev))
    def _():
        got_fwd[...] = jnp.zeros(got_fwd.shape, F32)

    loads[0].wait()
    loads[1].wait()
    cells = cells_v[...]
    count = cells.shape[1]
    row_of = lax.shift_right_logical(cells, 8)
    col_of = lax.bitwise_and(cells, 255)
    at_row = iota((R, count), 0) == row_of
    at_col = jnp.where(iota((C, count), 0) == col_of, 1.0, 0.0).astype(BF16)
    spread = []
    for f in range(3):
        rest = ow_v[f]
        for _ in range(3):
            part = rest.astype(BF16).astype(F32)
            rest = rest - part
            spread.append(jnp.where(at_row, part, 0.0).astype(BF16))
    sums = lax.dot_general(
        jnp.concatenate(spread, axis=0), at_col, (((1,), (1,)), ((), ())), preferred_element_type=F32
    )
    for f in range(3):
        top, low, rest = (sums[R * (3 * f + p) : R * (3 * f + p + 1)] for p in range(3))
        w_ext[f, 0:R, 0:C] = top + low + rest

    for load in loads[2:]:
        load.wait()
    mix = [[rea_s[f, 0, g] + (KEEP if f == g else 0.0) for g in range(3)] for f in range(3)]

    lane = iota((R, 128), 1)
    packed = jnp.zeros((R, 128), F32)
    own = [(x_ext, 0), (x_ext, 1), (x_ext, 2), (u_ext, 0), (u_ext, 1), (w_ext, 0), (w_ext, 1), (w_ext, 2), (mw_v, 0), (mw_v, 1), (mw_v, 2), (x_ext, 0), (x_ext, 1), (x_ext, 2)]
    for a, (ref, f) in enumerate(own):
        ends = jnp.where(lane < 64, ref[f, 0:R, 0:128], ref[f, 0:R, C - 128 : C])
        packed = jnp.where((lane >= 8 * a) & (lane < 8 * a + 8), rolled(ends, 8 * a + 4, 1), packed)
    pack[...] = packed
    half = R // 2
    low_lane = lax.rem(iota((half, 128), 1), 8) < 4
    left = iota((half // 2, 128), 1) < 64
    for e, pair in enumerate((
        jnp.where(low_lane, packed[:half], rolled(packed[half:], 4, 1)),
        jnp.where(low_lane, rolled(packed[half:], -4, 1), packed[:half]),
    )):
        upper, lower = pair[: half // 2], pair[half // 2 :]
        cols[0, e] = jnp.where(left, upper, rolled(lower, 64, 1))
        cols[1, e] = jnp.where(left, rolled(upper, 64, 1), lower)

    sub = iota((8, C), 0)
    lu, lv = u_ext[0, R - 8 : R, 0:C], u_ext[1, R - 8 : R, 0:C]
    fu, fv = u_ext[0, 0:8, 0:C], u_ext[1, 0:8, 0:C]
    for f in range(3):
        wind = jnp.where(sub == 1, rolled(lv, -4 - f, 0), rolled(lu, -5 - f, 0))
        obs = rolled(w_ext[f, R - 8 : R, 0:C], 4, 0)
        rows_own[0, f] = jnp.where(sub >= 4, x_ext[f, R - 8 : R, 0:C], jnp.where(sub >= 2, obs, wind))
        wind = jnp.where(sub == 6, rolled(fu, 6 - f, 0), rolled(fv, 7 - f, 0))
        obs = rolled(w_ext[f, 0:8, 0:C], 4, 0)
        rows_own[1, f] = jnp.where(sub < 4, x_ext[f, 0:8, 0:C], jnp.where(sub < 6, obs, wind))
    for pair in range(2):
        n_rows = n_cols = None
        for f in range(2 * pair, min(3, 2 * pair + 2)):
            base = 4 * (f % 2)
            lx, lm = x_ext[f, R - 8 : R, 0:C], mw_v[f, R - 8 : R, 0:C]
            fx, fm = x_ext[f, 0:8, 0:C], mw_v[f, 0:8, 0:C]
            top = jnp.where(lax.rem(sub, 4) >= 2, rolled(lx, -base, 0), rolled(lm, -base - 2, 0))
            bottom = jnp.where(lax.rem(sub, 4) < 2, rolled(fx, base, 0), rolled(fm, base + 2, 0))
            n_rows = top if n_rows is None else jnp.where(sub < 4, top, n_rows)
            n_cols = bottom if n_cols is None else jnp.where(sub >= 4, bottom, n_cols)
        rows_far[0, pair] = n_rows
        rows_far[1, pair] = n_cols

    lats = 1 + lat_ok(1).astype(jnp.int32) + lat_ok(-1).astype(jnp.int32)
    prev, nxt = has_prev.astype(jnp.int32), has_next.astype(jnp.int32)
    ends = (is_last(lat, lon) | is_first(lat, lon)).astype(jnp.int32)
    meets = meets_origin(win, lat, lon).astype(jnp.int32)
    knows_origin = (win < 2) & (lat == 0) & (lon == n_lon - 2)
    asks = owed = jnp.int32(0)
    for d, (dlat, dlon) in enumerate(DIRS):
        asks += (lat_ok(dlat) & answered(win, lat, lon, d)).astype(jnp.int32)
        owed += (lat_ok(-dlat) & answered(win + 1, lat - dlat, lon_at(-dlon), d)).astype(jnp.int32)
    fed = functools.reduce(jnp.add, [feed.astype(jnp.int32) for feed in feeds.values()])
    corner = is_corner(lat, lon).astype(jnp.int32)
    others = (3 * lats - 2 * ends - 4 * corner - asks) * (1 + prev) - 1 + nxt + owed * nxt
    pl.semaphore_wait(barrier, others - meets + knows_origin.astype(jnp.int32) + fed)

    def feed_message(d):
        dlat, dlon = DIRS[d]
        if dlon == 0:
            src, dst = rows_own.at[d], prev_rows.at[d]
        elif dlat == 0:
            src, dst = cols.at[0, d - 2], prev_cols.at[d - 2]
        else:
            src, dst = pack.at[pl.ds(R - 8 if dlat == 1 else 0, 8)], prev_corner.at[d - 4]
        return pltpu.make_async_remote_copy(
            src_ref=src,
            dst_ref=dst,
            send_sem=fsend_sem.at[d],
            recv_sem=frecv_sem.at[d],
            device_id=(win + 1, lat + dlat, lon_at(dlon)),
            device_id_type=MESH,
        )

    def message(d, dw):
        dlat, dlon = DIRS[d]
        if dlon == 0:
            src, dst = (rows_far.at[d], got_rows_far.at[d]) if dw else (rows_own.at[d], got_rows_own.at[d])
        elif dlat == 0:
            src, dst = cols.at[dw, d - 2], got_cols.at[dw, d - 2]
        else:
            src, dst = pack.at[pl.ds(R - 8 if dlat == 1 else 0, 8)], got_corner.at[dw, d - 4]
        return pltpu.make_async_remote_copy(
            src_ref=src,
            dst_ref=dst,
            send_sem=send_sem.at[dw, d],
            recv_sem=recv_sem.at[dw, d],
            device_id=(win - dw, lat + dlat, lon_at(dlon)),
            device_id_type=MESH,
        )

    def across(i, src, dst, step):
        return pltpu.make_async_remote_copy(
            src_ref=src,
            dst_ref=dst,
            send_sem=xsend_sem.at[i],
            recv_sem=xrecv_sem.at[i],
            device_id=(win + step, lat, lon),
            device_id_type=MESH,
        )

    def copies(dw):
        for d, (dlat, _) in enumerate(DIRS):
            yield d, lat_ok(dlat) & (has_prev if dw else (win >= 0)), lat_ok(-dlat) & (has_next if dw else (win >= 0))

    def answer():
        for dw in range(2):
            for d, _, ok in copies(dw):
                dlat, dlon = DIRS[d]
                source = (win + dw, lat - dlat, lon_at(-dlon))


                @pl.when(ok & answered(*source, d))
                def _(source=source):
                    pl.semaphore_signal(far_ok, inc=1, device_id=source, device_id_type=MESH)

    for now in range(3):
        for dw in range(2):
            for d, ok, _ in copies(dw):

                @pl.when(ok & (turn(d) == now) & jnp.logical_not(deferred(win, lat, lon, d, dw) | answered(win, lat, lon, d)))
                def _(d=d, dw=dw):
                    message(d, dw).start()

        if now == 0:
            answer()

    bulk = [across(0, inc_h.at[0], inc_n, -1), across(1, mw_h.at[0], mw_n, -1)]
    first = across(2, fwd0, got_fwd, 1)
    late = [across(3, ring_r, got_ring_r, 1), across(4, ring_c, got_ring_c, 1)]
    origin_own = [across(5, inc_h.at[0], prev_inc, 1), across(6, winds_h.at[0], prev_wind, 1), across(7, rea_h, prev_rea, 1)]
    to_next = has_next & jnp.logical_not(origin)
    from_prev = has_prev & jnp.logical_not(follower)

    for d, feed in feeds.items():

        @pl.when(feed)
        def _(d=d):
            feed_message(d).start()

    @pl.when(origin & has_next)
    def _():
        for copy in origin_own:
            copy.start()

    @pl.when(((lat == mid - 1) | (lat == mid)) & (lon == n_lon - 2))
    def _():
        pl.semaphore_signal(gate, inc=1, device_id=(win, lat, lon + 1), device_id_type=MESH)

    @pl.when(knows_origin)
    def _():
        pl.semaphore_signal(gate, inc=1, device_id=(win, lat, lon + 1), device_id_type=MESH)
        pl.semaphore_signal(gate, inc=1, device_id=(win, lat + 1, lon + 1), device_id_type=MESH)

    @pl.when((lat == mid + 1) & ((lon == 0) | (lon == n_lon - 1)))
    def _():
        pl.semaphore_signal(gate, inc=1, device_id=(win, lat - 1, lon), device_id_type=MESH)

    uc, vc = u_ext[0, 0:R, 0:C], u_ext[1, 0:R, 0:C]
    coef[0, 0:R, 0:C] = DIFFUSION - uc
    coef[1, 0:R, 0:C] = DIFFUSION + uc
    coef[2, 0:R, 0:C] = DIFFUSION - vc
    coef[3, 0:R, 0:C] = DIFFUSION + vc
    c_tile = [coef[i, 0:R, 0:C] for i in range(4)]
    state = [x_ext[f, 0:R, 0:C] for f in range(3)]
    for _ in range(2):
        state = tangent(state, c_tile, mix)
    for f in range(3):
        fwd0[f] = state[f]

    @pl.when(to_next)
    def _():
        first.start()

    @pl.when(has_prev)
    def _():
        bulk[0].start()
        bulk[1].start()

    @pl.when(ends + meets + corner > 0)
    def _():
        pl.semaphore_wait(gate, ends + meets + 2 * corner)
        for dw in range(2):
            for d, ok, _ in copies(dw):

                @pl.when(ok & deferred(win, lat, lon, d, dw))
                def _(d=d, dw=dw):
                    message(d, dw).start()

    @pl.when(asks > 0)
    def _():
        pl.semaphore_wait(far_ok, asks * (1 + prev))
        for dw in range(2):
            for d, ok, _ in copies(dw):

                @pl.when(ok & answered(win, lat, lon, d))
                def _(d=d, dw=dw):
                    message(d, dw).start()

    def arrive(dw):
        for d, _, ok in copies(dw):

            @pl.when(ok)
            def _(d=d, dw=dw):
                message(d, dw).wait_recv()

    arrive(0)

    corner_low = lax.rem(iota((8, 128), 1), 8) < 4
    corner_sub = iota((8, 128), 0)

    def columns(from_cols, from_corner, far):
        from_west, from_east = (
            jnp.concatenate([from_cols[i], rolled(from_cols[i], 64, 1)], axis=0) for i in range(2)
        )
        upper = jnp.where(low_lane, from_west, from_east)
        lower = jnp.where(low_lane, rolled(from_west, -4, 1), rolled(from_east, 4, 1))
        sw, se, nw, ne = (from_corner[i] for i in range(4))
        rim = jnp.where(corner_sub < 4, jnp.where(corner_low, nw, ne), jnp.where(corner_low, sw, se))
        return jnp.concatenate([upper, lower, rolled(rim, 64, 1) if far else rim], axis=0)

    own_cols = columns(got_cols.at[0], got_corner.at[0], False)

    def side(ends, a):
        return rolled(ends, -8 * a - 4, 1)

    E = R + 8
    inside = jnp.where(iota((8, C), 0) < 4, lat_ok(1).astype(F32), lat_ok(-1).astype(F32)) > 0.0
    def unpack(from_rows, ends_all, x, c):
        for f in range(3):
            x[f, :, C:] = side(ends_all, f)
            x[f, R:E, 0:C] = jnp.where(sub < 4, from_rows[1, f], from_rows[0, f])
        for i in range(2):
            rows = jnp.zeros((8, C), F32)
            for t in range(3):
                rows = jnp.where(sub == t, rolled(from_rows[1, t], t - 6 - i, 0), rows)
                rows = jnp.where(sub == 5 + t, rolled(from_rows[0, t], 5 + t - i, 0), rows)
            c[2 * i, R:E, 0:C] = jnp.where(inside, DIFFUSION - rows, 0.0)
            c[2 * i + 1, R:E, 0:C] = jnp.where(inside, DIFFUSION + rows, 0.0)
            ends = side(ends_all, 3 + i)
            less, more = DIFFUSION - ends, DIFFUSION + ends
            c[2 * i, 0:R, C:] = less[0:R]
            c[2 * i + 1, 0:R, C:] = more[0:R]
            c[2 * i, R:E, C:] = jnp.where(inside[:, 0:128], less[R:E], 0.0)
            c[2 * i + 1, R:E, C:] = jnp.where(inside[:, 0:128], more[R:E], 0.0)

    unpack(got_rows_own, own_cols, x_ext, coef)
    for f in range(3):
        w_ext[f, :, C:] = side(own_cols, 5 + f)
        w_ext[f, R:E, 0:C] = rolled(jnp.where(sub < 4, got_rows_own[0, f], got_rows_own[1, f]), 4, 0)

    c_all = [coef[i] for i in range(4)]
    state = tangent([x_ext[f] for f in range(3)], c_all, mix)
    for f in range(3):
        t_ext[f] = state[f]
    state = tangent([t_ext[f] for f in range(3)], c_all, mix)

    ring = jnp.zeros((R, 128), F32)
    for f in range(3):
        t_ext[f] = state[f]
        ring_r[f] = jnp.where(sub < 4, t_ext[f, 0:8, 0:C], t_ext[f, R - 8 : R, 0:C])
        ends = jnp.where(lane < 64, t_ext[f, 0:R, 0:128], t_ext[f, 0:R, C - 128 : C])
        ring = jnp.where((lane >= 8 * f) & (lane < 8 * f + 8), rolled(ends, 8 * f + 4, 1), ring)
    quarter = R // 4
    folded = ring[0:quarter]
    group = iota((quarter, 128), 1)
    for q in range(1, 4):
        folded = jnp.where(group >= 32 * q, rolled(ring[quarter * q : quarter * (q + 1)], 32 * q, 1), folded)
    ring_c[...] = folded

    @pl.when(to_next)
    def _():
        late[0].start()
        late[1].start()

    arrive(1)
    far_cols = columns(got_cols.at[1], got_corner.at[1], True)

    @pl.when(has_next)
    def _():
        bulk[0].wait_recv()
        bulk[1].wait_recv()

    for f in range(3):
        t, base = f // 2, 4 * (f % 2)
        south_rows, north_rows = got_rows_far[0, t], got_rows_far[1, t]
        inc_rows = jnp.where(sub < 4, rolled(north_rows, -base, 0), rolled(south_rows, base, 0))
        mw_rows = jnp.where(sub < 4, rolled(north_rows, -base - 2, 0), rolled(south_rows, base + 2, 0))
        mw_cols = side(far_cols, f)
        g_ext[f, 0:R, 0:C] = w_ext[f, 0:R, 0:C] + mw_n[f]
        h_ext[f, 0:R, 0:C] = mw_n[f] * inc_n[f]
        g_ext[f, R:E, 0:C] = w_ext[f, R:E, 0:C] + mw_rows
        h_ext[f, R:E, 0:C] = mw_rows * inc_rows
        g_ext[f, :, C:] = w_ext[f, :, C:] + mw_cols
        h_ext[f, :, C:] = mw_cols * side(far_cols, 3 + f)

    state = [g_ext[f] * t_ext[f] - h_ext[f] for f in range(3)]
    state = adjoint(state, c_all, mix)
    for f in range(3):
        h_ext[f] = state[f]
    state = adjoint([h_ext[f] for f in range(3)], c_all, mix)
    for f in range(3):
        h_ext[f] = state[f]

    @pl.when(follower)
    def _():
        for copy in origin_own:
            copy.wait_recv()
        reaction = pltpu.make_async_copy(prev_rea, prev_rea_s, load_sem.at[6])
        reaction.start()
        for d in feeds:
            feed_message(d).wait_recv()
        for f in range(3):
            xp_ext[f, 0:R, 0:C] = prev_inc[f]
        for i in range(2):
            cp_ext[2 * i, 0:R, 0:C] = DIFFUSION - prev_wind[i]
            cp_ext[2 * i + 1, 0:R, 0:C] = DIFFUSION + prev_wind[i]
        unpack(prev_rows, columns(prev_cols, prev_corner, False), xp_ext, cp_ext)
        reaction.wait()
        prev_mix = [[prev_rea_s[f, 0, g] + (KEEP if f == g else 0.0) for g in range(3)] for f in range(3)]
        c_prev = [cp_ext[i] for i in range(4)]
        state = tangent([xp_ext[f] for f in range(3)], c_prev, prev_mix)
        for f in range(3):
            xp_ext[f] = state[f]
        state = tangent([xp_ext[f] for f in range(3)], c_prev, prev_mix)
        for f in range(3):
            got_fwd[f] = state[f][0:R, 0:C]

    @pl.when(from_prev)
    def _():
        first.wait_recv()
        late[0].wait_recv()
        late[1].wait_recv()
        folded = got_ring_c[...]
        ring = jnp.concatenate([rolled(folded, -32 * q, 1) for q in range(4)], axis=0)
        for f in range(3):
            rows = got_ring_r[f]
            got_fwd[f, 0:8] = jnp.where(sub < 2, rows, got_fwd[f, 0:8])
            got_fwd[f, R - 8 : R] = jnp.where(sub >= 6, rows, got_fwd[f, R - 8 : R])
            ends = rolled(ring, -8 * f - 4, 1)
            got_fwd[f, :, 0:128] = jnp.where(lane < 2, ends, got_fwd[f, :, 0:128])
            got_fwd[f, :, C - 128 : C] = jnp.where(lane >= 126, ends, got_fwd[f, :, C - 128 : C])

    for f in range(3):
        out_ref[0, f] = mw_v[f] * (x_ext[f, 0:R, 0:C] - got_fwd[f]) + h_ext[f, 0:R, 0:C]

    for dw in range(2):
        for d, ok, _ in copies(dw):

            @pl.when(ok)
            def _(d=d, dw=dw):
                message(d, dw).wait_send()

    @pl.when(to_next)
    def _():
        first.wait_send()
        late[0].wait_send()
        late[1].wait_send()

    for d, feed in feeds.items():

        @pl.when(feed)
        def _(d=d):
            feed_message(d).wait_send()

    @pl.when(origin & has_next)
    def _():
        for copy in origin_own:
            copy.wait_send()

    @pl.when(has_prev)
    def _():
        bulk[0].wait_send()
        bulk[1].wait_send()


def per_device(sizes, *args):
    args = args[:3] + (jnp.transpose(args[3], (1, 0, 2)),) + args[4:]
    R, C = args[0].shape[-2:]
    count = args[4].shape[-1]
    args = [pltpu.with_memory_space_constraint(a, pltpu.HBM) for a in args]
    ext = (R + 8, C + 128)
    vmem = lambda *shape: pltpu.VMEM(shape, F32)
    anywhere = pl.BlockSpec(memory_space=pl.ANY)
    return pl.pallas_call(
        functools.partial(kernel, sizes),
        out_shape=jax.ShapeDtypeStruct(args[0].shape, F32),
        in_specs=[anywhere] * 6,
        out_specs=pl.BlockSpec(memory_space=pltpu.VMEM),
        scratch_shapes=[
            vmem(3, *ext), vmem(2, *ext), vmem(3, *ext), vmem(4, *ext), vmem(3, *ext), vmem(3, *ext), vmem(3, *ext),
            vmem(3, R, C), pltpu.SMEM((3, 1, 3), F32), pltpu.VMEM((1, count), jnp.int32), vmem(3, 1, count),
            vmem(R, 128), vmem(2, 2, R // 4, 128), vmem(2, 3, 8, C), vmem(2, 2, 8, C),
            vmem(3, R, C), vmem(3, 8, C), vmem(R // 4, 128),
            vmem(2, 3, 8, C), vmem(2, 2, 8, C), vmem(2, 2, R // 4, 128), vmem(2, 4, 8, 128),
            vmem(3, R, C), vmem(3, R, C), vmem(3, R, C), vmem(3, 8, C), vmem(R // 4, 128),
            pltpu.SemaphoreType.DMA((7,)), pltpu.SemaphoreType.DMA((2, 8)), pltpu.SemaphoreType.DMA((2, 8)),
            pltpu.SemaphoreType.DMA((8,)), pltpu.SemaphoreType.DMA((8,)), pltpu.SemaphoreType.DMA((8,)), pltpu.SemaphoreType.DMA((8,)),
            pltpu.SemaphoreType.REGULAR, pltpu.SemaphoreType.REGULAR,
            vmem(2, 3, 8, C), vmem(2, R // 4, 128), vmem(4, 8, 128), vmem(3, R, C), vmem(2, R, C), vmem(3, 1, 3),
            pltpu.SMEM((3, 1, 3), F32), vmem(3, *ext), vmem(4, *ext),
        ],
        compiler_params=pltpu.CompilerParams(
            collective_id=0, has_side_effects=True, vmem_limit_bytes=32 * 1024 * 1024
        ),
        cost_estimate=pl.CostEstimate(flops=10_000_000, bytes_accessed=1_000_000, transcendentals=0),
        name="window_product",
    )(*args)


def solution(mesh):
    sizes = tuple(mesh.shape[name] for name in ("win", "lat", "lon"))
    in_specs = (
        P("win", None, "lat", "lon"),
        P("win", None, "lat", "lon"),
        P("win", None, "lat", "lon"),
        P("win", None, None),
        P("win", "lat", "lon", None),
        P("win", None, "lat", "lon", None),
    )
    out_specs = P("win", None, "lat", "lon")
    return jax.shard_map(
        functools.partial(per_device, sizes), mesh=mesh, in_specs=in_specs, out_specs=out_specs, check_vma=False
    )
```

```python
import functools

import jax
import jax.numpy as jnp
from jax import lax
from jax.experimental import pallas as pl
from jax.experimental.pallas import tpu as pltpu
from jax.sharding import PartitionSpec as P

DIFFUSION = 0.15
KEEP = 1.0 - 4.0 * DIFFUSION
MESH = pl.DeviceIdType.MESH
F32 = jnp.float32
BF16 = jnp.bfloat16
DIRS = ((1, 0), (-1, 0), (0, 1), (0, -1), (1, 1), (1, -1), (-1, 1), (-1, -1))


def rolled(x, shift, axis):
    shift = shift % x.shape[axis]
    return x if shift == 0 else pltpu.roll(x, shift, axis)


def east(x):
    return rolled(x, -1, 1)


def west(x):
    return rolled(x, 1, 1)


def north(x):
    return rolled(x, -1, 0)


def south(x):
    return rolled(x, 1, 0)


def tangent(xs, coef, mix):
    a, b, c, d = coef
    out = []
    for f in range(3):
        x = xs[f]
        y = a * east(x) + b * west(x) + c * north(x) + d * south(x)
        out.append(y + mix[f][0] * xs[0] + mix[f][1] * xs[1] + mix[f][2] * xs[2])
    return out


def adjoint(zs, coef, mix):
    a, b, c, d = coef
    out = []
    for f in range(3):
        z = zs[f]
        y = east(b * z) + west(a * z) + north(d * z) + south(c * z)
        out.append(y + mix[0][f] * zs[0] + mix[1][f] * zs[1] + mix[2][f] * zs[2])
    return out


def iota(shape, axis):
    return lax.broadcasted_iota(jnp.int32, shape, axis)


def kernel(
    sizes,
    inc_h, mw_h, winds_h, rea_h, cells_h, ow_h,
    out_ref,
    x_ext, u_ext, w_ext, coef, g_ext, h_ext, t_ext,
    mw_v, rea_s, cells_v, ow_v,
    pack, cols, rows_own, rows_far, fwd0, ring_r, ring_c,
    got_rows_own, got_rows_far, got_cols, got_corner, inc_n, mw_n, got_fwd, got_ring_r, got_ring_c,
    load_sem, send_sem, recv_sem, xsend_sem, xrecv_sem, fsend_sem, frecv_sem, gate, far_ok,
    prev_rows, prev_cols, prev_corner, prev_inc, prev_wind, prev_rea, prev_rea_s, xp_ext, cp_ext,
):
    n_win, n_lat, n_lon = sizes
    win, lat, lon = lax.axis_index("win"), lax.axis_index("lat"), lax.axis_index("lon")
    R, C = 64, 256

    def lon_at(step):
        return lax.rem(lon + step + n_lon, n_lon)

    def lat_ok(step):
        return (lat + step >= 0) & (lat + step < n_lat)

    has_prev, has_next = win > 0, win < n_win - 1
    mid = n_lat // 2

    def is_last(at_lat, at_lon):
        return (at_lat == mid - 1) & (at_lon == n_lon - 1)

    def is_first(at_lat, at_lon):
        return (at_lat == mid) & (at_lon == 0)

    def is_corner(at_lat, at_lon):
        return (at_lat == mid) & (at_lon == n_lon - 1)

    def meets_origin(at_win, at_lat, at_lon):
        return (at_win < 2) & (at_lat < 2) & (at_lon == n_lon - 1)

    def deferred(at_win, at_lat, at_lon, d, dw):
        dlat, dlon = DIRS[d]
        held = lat < 0
        if dlat == 1 and dlon <= 0:
            held = held | is_last(at_lat, at_lon)
        if dlon == -1 and dlat >= 0:
            held = held | is_first(at_lat, at_lon)
        if (dlat == -1 and dlon <= 0) or (dlon == 1 and dlat >= 0):
            held = held | is_corner(at_lat, at_lon)
        if dlon == 1 and dlat <= 0:
            held = held | ((at_win == dw) & (at_lat == -dlat) & (at_lon == n_lon - 1))
        return held

    def answered(at_win, at_lat, at_lon, d):
        dlat, dlon = DIRS[d]
        early = lat < 0
        if dlon == -1:
            early = early | ((at_lon == 0) & (at_lat < mid) & (at_lat + dlat < mid))
        if dlat == 1:
            early = early | ((at_lat == mid - 1) & (at_lon < n_lon // 2))
        return early & ((at_win > 0) | (at_lat > 0) | (at_lon > 0))

    def turn(d):
        dlat, dlon = DIRS[d]
        urgent = later = lat < 0
        if dlat == -1:
            urgent = urgent | (lat == mid)
        if dlon == 1:
            urgent = urgent | (lon == n_lon - 1)
        if dlat == 1:
            later = later | (lat == mid - 1)
        if dlon == -1:
            later = later | (lon == 0)
        return jnp.where(urgent, 0, jnp.where(later, 2, 1))

    barrier = pltpu.get_barrier_semaphore()

    def tell(ok, target):
        @pl.when(ok)
        def _():
            pl.semaphore_signal(barrier, inc=1, device_id=target, device_id_type=MESH)

    def is_near(d):
        dlat, dlon = DIRS[d]
        cut = lat < 0
        if dlat:
            cut = cut | (lat == (mid if dlat == 1 else mid - 1))
        if dlon:
            cut = cut | (lon == (0 if dlon == 1 else n_lon - 1))
        return jnp.logical_not(cut)

    for d, (dlat, dlon) in enumerate(DIRS):
        for dw in range(2):
            source = (win + dw, lat - dlat, lon_at(-dlon))
            ok = lat_ok(-dlat) & jnp.logical_not(deferred(*source, d, dw) | answered(*source, d))
            tell((ok & has_next if dw else ok) & is_near(d), source)
    origin = (win == 0) & (lat == 0) & (lon == 0)
    follower = (win == 1) & (lat == 0) & (lon == 0)
    feeds = {
        d: has_next & (win == 0) & (lat == -dlat) & (lon_at(dlon) == 0)
        for d, (dlat, dlon) in enumerate(DIRS)
        if dlat <= 0
    }
    for d in feeds:
        tell(follower, (win - 1, lat - DIRS[d][0], lon_at(-DIRS[d][1])))
    tell(origin, (win, lat, lon_at(-2)))
    tell(origin & has_next, (win + 1, lat, lon_at(-2)))
    tell(has_next, (win + 1, lat, lon))
    tell(has_prev, (win - 1, lat, lon))

    tile = (slice(None), pl.ds(0, R), pl.ds(0, C))
    loads = [
        pltpu.make_async_copy(cells_h.at[0, 0], cells_v, load_sem.at[0]),
        pltpu.make_async_copy(ow_h.at[0, :, 0], ow_v, load_sem.at[1]),
        pltpu.make_async_copy(inc_h.at[0], x_ext.at[tile], load_sem.at[2]),
        pltpu.make_async_copy(winds_h.at[0], u_ext.at[tile], load_sem.at[3]),
        pltpu.make_async_copy(mw_h.at[0], mw_v, load_sem.at[4]),
        pltpu.make_async_copy(rea_h, rea_s, load_sem.at[5]),
    ]
    for load in loads:
        load.start()

    for d, (dlat, dlon) in enumerate(DIRS):
        for dw in range(2):
            source = (win + dw, lat - dlat, lon_at(-dlon))
            ok = lat_ok(-dlat) & jnp.logical_not(deferred(*source, d, dw) | answered(*source, d))
            tell((ok & has_next if dw else ok) & jnp.logical_not(is_near(d)), source)
        tell(has_prev & lat_ok(dlat) & answered(win, lat, lon, d), (win - 1, lat + dlat, lon_at(dlon)))

    for d, (dlat, dlon) in enumerate(DIRS):
        for dw in range(2):
            there = lat_ok(-dlat) & (has_next if dw else (win >= 0))

            @pl.when(jnp.logical_not(there))
            def _(d=d, dw=dw, dlat=dlat, dlon=dlon):
                if dlon == 0:
                    ref = got_rows_far.at[d] if dw else got_rows_own.at[d]
                elif dlat == 0:
                    ref = got_cols.at[dw, d - 2]
                else:
                    ref = got_corner.at[dw, d - 4]
                ref[...] = jnp.zeros(ref.shape, F32)

    @pl.when(follower)
    def _():
        prev_rows[0] = jnp.zeros(prev_rows.shape[1:], F32)
        for i, (dlat, _) in enumerate(DIRS[4:]):
            if dlat > 0:
                prev_corner[i] = jnp.zeros(prev_corner.shape[1:], F32)

    @pl.when(jnp.logical_not(has_next))
    def _():
        inc_n[...] = jnp.zeros(inc_n.shape, F32)
        mw_n[...] = jnp.zeros(mw_n.shape, F32)

    @pl.when(jnp.logical_not(has_prev))
    def _():
        got_fwd[...] = jnp.zeros(got_fwd.shape, F32)

    loads[0].wait()
    loads[1].wait()
    cells = cells_v[...]
    count = cells.shape[1]
    row_of = lax.shift_right_logical(cells, 8)
    col_of = lax.bitwise_and(cells, 255)
    at_row = iota((R, count), 0) == row_of
    at_col = jnp.where(iota((C, count), 0) == col_of, 1.0, 0.0).astype(BF16)
    spread = []
    for f in range(3):
        rest = ow_v[f]
        for _ in range(3):
            part = rest.astype(BF16).astype(F32)
            rest = rest - part
            spread.append(jnp.where(at_row, part, 0.0).astype(BF16))
    sums = lax.dot_general(
        jnp.concatenate(spread, axis=0), at_col, (((1,), (1,)), ((), ())), preferred_element_type=F32
    )
    for f in range(3):
        top, low, rest = (sums[R * (3 * f + p) : R * (3 * f + p + 1)] for p in range(3))
        w_ext[f, 0:R, 0:C] = top + low + rest

    for load in loads[2:]:
        load.wait()
    mix = [[rea_s[f, 0, g] + (KEEP if f == g else 0.0) for g in range(3)] for f in range(3)]

    sub = iota((8, C), 0)
    lu, lv = u_ext[0, R - 8 : R, 0:C], u_ext[1, R - 8 : R, 0:C]
    fu, fv = u_ext[0, 0:8, 0:C], u_ext[1, 0:8, 0:C]
    for f in range(3):
        wind = jnp.where(sub == 1, rolled(lv, -4 - f, 0), rolled(lu, -5 - f, 0))
        obs = rolled(w_ext[f, R - 8 : R, 0:C], 4, 0)
        rows_own[0, f] = jnp.where(sub >= 4, x_ext[f, R - 8 : R, 0:C], jnp.where(sub >= 2, obs, wind))
        wind = jnp.where(sub == 6, rolled(fu, 6 - f, 0), rolled(fv, 7 - f, 0))
        obs = rolled(w_ext[f, 0:8, 0:C], 4, 0)
        rows_own[1, f] = jnp.where(sub < 4, x_ext[f, 0:8, 0:C], jnp.where(sub < 6, obs, wind))
    for pair in range(2):
        n_rows = n_cols = None
        for f in range(2 * pair, min(3, 2 * pair + 2)):
            base = 4 * (f % 2)
            lx, lm = x_ext[f, R - 8 : R, 0:C], mw_v[f, R - 8 : R, 0:C]
            fx, fm = x_ext[f, 0:8, 0:C], mw_v[f, 0:8, 0:C]
            top = jnp.where(lax.rem(sub, 4) >= 2, rolled(lx, -base, 0), rolled(lm, -base - 2, 0))
            bottom = jnp.where(lax.rem(sub, 4) < 2, rolled(fx, base, 0), rolled(fm, base + 2, 0))
            n_rows = top if n_rows is None else jnp.where(sub < 4, top, n_rows)
            n_cols = bottom if n_cols is None else jnp.where(sub >= 4, bottom, n_cols)
        rows_far[0, pair] = n_rows
        rows_far[1, pair] = n_cols

    lane = iota((R, 128), 1)
    packed = jnp.zeros((R, 128), F32)
    own = [(x_ext, 0), (x_ext, 1), (x_ext, 2), (u_ext, 0), (u_ext, 1), (w_ext, 0), (w_ext, 1), (w_ext, 2), (mw_v, 0), (mw_v, 1), (mw_v, 2), (x_ext, 0), (x_ext, 1), (x_ext, 2)]
    for a, (ref, f) in enumerate(own):
        ends = jnp.where(lane < 64, ref[f, 0:R, 0:128], ref[f, 0:R, C - 128 : C])
        packed = jnp.where((lane >= 8 * a) & (lane < 8 * a + 8), rolled(ends, 8 * a + 4, 1), packed)
    pack[...] = packed
    half = R // 2
    low_lane = lax.rem(iota((half, 128), 1), 8) < 4
    left = iota((half // 2, 128), 1) < 64
    for e, pair in enumerate((
        jnp.where(low_lane, packed[:half], rolled(packed[half:], 4, 1)),
        jnp.where(low_lane, rolled(packed[half:], -4, 1), packed[:half]),
    )):
        upper, lower = pair[: half // 2], pair[half // 2 :]
        cols[0, e] = jnp.where(left, upper, rolled(lower, 64, 1))
        cols[1, e] = jnp.where(left, rolled(upper, 64, 1), lower)

    lats = 1 + lat_ok(1).astype(jnp.int32) + lat_ok(-1).astype(jnp.int32)
    prev, nxt = has_prev.astype(jnp.int32), has_next.astype(jnp.int32)
    ends = (is_last(lat, lon) | is_first(lat, lon)).astype(jnp.int32)
    meets = meets_origin(win, lat, lon).astype(jnp.int32)
    knows_origin = (win < 2) & (lat == 0) & (lon == n_lon - 2)
    asks = owed = jnp.int32(0)
    for d, (dlat, dlon) in enumerate(DIRS):
        asks += (lat_ok(dlat) & answered(win, lat, lon, d)).astype(jnp.int32)
        owed += (lat_ok(-dlat) & answered(win + 1, lat - dlat, lon_at(-dlon), d)).astype(jnp.int32)
    fed = functools.reduce(jnp.add, [feed.astype(jnp.int32) for feed in feeds.values()])
    corner = is_corner(lat, lon).astype(jnp.int32)
    others = (3 * lats - 2 * ends - 4 * corner - asks) * (1 + prev) - 1 + nxt + owed * nxt
    pl.semaphore_wait(barrier, others - meets + knows_origin.astype(jnp.int32) + fed)

    def feed_message(d):
        dlat, dlon = DIRS[d]
        if dlon == 0:
            src, dst = rows_own.at[d], prev_rows.at[d]
        elif dlat == 0:
            src, dst = cols.at[0, d - 2], prev_cols.at[d - 2]
        else:
            src, dst = pack.at[pl.ds(R - 8 if dlat == 1 else 0, 8)], prev_corner.at[d - 4]
        return pltpu.make_async_remote_copy(
            src_ref=src,
            dst_ref=dst,
            send_sem=fsend_sem.at[d],
            recv_sem=frecv_sem.at[d],
            device_id=(win + 1, lat + dlat, lon_at(dlon)),
            device_id_type=MESH,
        )

    def message(d, dw):
        dlat, dlon = DIRS[d]
        if dlon == 0:
            src, dst = (rows_far.at[d], got_rows_far.at[d]) if dw else (rows_own.at[d], got_rows_own.at[d])
        elif dlat == 0:
            src, dst = cols.at[dw, d - 2], got_cols.at[dw, d - 2]
        else:
            src, dst = pack.at[pl.ds(R - 8 if dlat == 1 else 0, 8)], got_corner.at[dw, d - 4]
        return pltpu.make_async_remote_copy(
            src_ref=src,
            dst_ref=dst,
            send_sem=send_sem.at[dw, d],
            recv_sem=recv_sem.at[dw, d],
            device_id=(win - dw, lat + dlat, lon_at(dlon)),
            device_id_type=MESH,
        )

    def across(i, src, dst, step):
        return pltpu.make_async_remote_copy(
            src_ref=src,
            dst_ref=dst,
            send_sem=xsend_sem.at[i],
            recv_sem=xrecv_sem.at[i],
            device_id=(win + step, lat, lon),
            device_id_type=MESH,
        )

    def copies(dw):
        for d, (dlat, _) in enumerate(DIRS):
            yield d, lat_ok(dlat) & (has_prev if dw else (win >= 0)), lat_ok(-dlat) & (has_next if dw else (win >= 0))

    def answer():
        for dw in range(2):
            for d, _, ok in copies(dw):
                dlat, dlon = DIRS[d]
                source = (win + dw, lat - dlat, lon_at(-dlon))


                @pl.when(ok & answered(*source, d))
                def _(source=source):
                    pl.semaphore_signal(far_ok, inc=1, device_id=source, device_id_type=MESH)

    for now in range(3):
        for dw in range(2):
            for d, ok, _ in copies(dw):

                @pl.when(ok & (turn(d) == now) & jnp.logical_not(deferred(win, lat, lon, d, dw) | answered(win, lat, lon, d)))
                def _(d=d, dw=dw):
                    message(d, dw).start()

        if now == 0:
            answer()

    bulk = [across(0, inc_h.at[0], inc_n, -1), across(1, mw_h.at[0], mw_n, -1)]
    first = across(2, fwd0, got_fwd, 1)
    late = [across(3, ring_r, got_ring_r, 1), across(4, ring_c, got_ring_c, 1)]
    origin_own = [across(5, inc_h.at[0], prev_inc, 1), across(6, winds_h.at[0], prev_wind, 1), across(7, rea_h, prev_rea, 1)]
    to_next = has_next & jnp.logical_not(origin)
    from_prev = has_prev & jnp.logical_not(follower)

    for d, feed in feeds.items():

        @pl.when(feed)
        def _(d=d):
            feed_message(d).start()

    @pl.when(origin & has_next)
    def _():
        for copy in origin_own:
            copy.start()

    @pl.when(((lat == mid - 1) | (lat == mid)) & (lon == n_lon - 2))
    def _():
        pl.semaphore_signal(gate, inc=1, device_id=(win, lat, lon + 1), device_id_type=MESH)

    @pl.when(knows_origin)
    def _():
        pl.semaphore_signal(gate, inc=1, device_id=(win, lat, lon + 1), device_id_type=MESH)
        pl.semaphore_signal(gate, inc=1, device_id=(win, lat + 1, lon + 1), device_id_type=MESH)

    @pl.when((lat == mid + 1) & ((lon == 0) | (lon == n_lon - 1)))
    def _():
        pl.semaphore_signal(gate, inc=1, device_id=(win, lat - 1, lon), device_id_type=MESH)

    uc, vc = u_ext[0, 0:R, 0:C], u_ext[1, 0:R, 0:C]
    coef[0, 0:R, 0:C] = DIFFUSION - uc
    coef[1, 0:R, 0:C] = DIFFUSION + uc
    coef[2, 0:R, 0:C] = DIFFUSION - vc
    coef[3, 0:R, 0:C] = DIFFUSION + vc
    c_tile = [coef[i, 0:R, 0:C] for i in range(4)]
    state = [x_ext[f, 0:R, 0:C] for f in range(3)]
    for _ in range(2):
        state = tangent(state, c_tile, mix)
    for f in range(3):
        fwd0[f] = state[f]

    @pl.when(to_next)
    def _():
        first.start()

    @pl.when(has_prev)
    def _():
        bulk[0].start()
        bulk[1].start()

    @pl.when(ends + meets + corner > 0)
    def _():
        pl.semaphore_wait(gate, ends + meets + 2 * corner)
        for dw in range(2):
            for d, ok, _ in copies(dw):

                @pl.when(ok & deferred(win, lat, lon, d, dw))
                def _(d=d, dw=dw):
                    message(d, dw).start()

    @pl.when(asks > 0)
    def _():
        pl.semaphore_wait(far_ok, asks * (1 + prev))
        for dw in range(2):
            for d, ok, _ in copies(dw):

                @pl.when(ok & answered(win, lat, lon, d))
                def _(d=d, dw=dw):
                    message(d, dw).start()

    def arrive(dw):
        for d, _, ok in copies(dw):

            @pl.when(ok)
            def _(d=d, dw=dw):
                message(d, dw).wait_recv()

    @pl.when(has_next)
    def _():
        bulk[0].wait_recv()
        bulk[1].wait_recv()

    for f in range(3):
        g_ext[f, 0:R, 0:C] = w_ext[f, 0:R, 0:C] + mw_n[f]
        h_ext[f, 0:R, 0:C] = mw_n[f] * inc_n[f]

    arrive(0)

    corner_low = lax.rem(iota((8, 128), 1), 8) < 4
    corner_sub = iota((8, 128), 0)

    def columns(from_cols, from_corner, far):
        from_west, from_east = (
            jnp.concatenate([from_cols[i], rolled(from_cols[i], 64, 1)], axis=0) for i in range(2)
        )
        upper = jnp.where(low_lane, from_west, from_east)
        lower = jnp.where(low_lane, rolled(from_west, -4, 1), rolled(from_east, 4, 1))
        sw, se, nw, ne = (from_corner[i] for i in range(4))
        rim = jnp.where(corner_sub < 4, jnp.where(corner_low, nw, ne), jnp.where(corner_low, sw, se))
        return jnp.concatenate([upper, lower, rolled(rim, 64, 1) if far else rim], axis=0)

    own_cols = columns(got_cols.at[0], got_corner.at[0], False)

    def side(ends, a):
        return rolled(ends, -8 * a - 4, 1)

    E = R + 8
    inside = jnp.where(iota((8, C), 0) < 4, lat_ok(1).astype(F32), lat_ok(-1).astype(F32)) > 0.0
    def unpack(from_rows, ends_all, x, c):
        for f in range(3):
            x[f, :, C:] = side(ends_all, f)
            x[f, R:E, 0:C] = jnp.where(sub < 4, from_rows[1, f], from_rows[0, f])
        for i in range(2):
            rows = jnp.zeros((8, C), F32)
            for t in range(3):
                rows = jnp.where(sub == t, rolled(from_rows[1, t], t - 6 - i, 0), rows)
                rows = jnp.where(sub == 5 + t, rolled(from_rows[0, t], 5 + t - i, 0), rows)
            c[2 * i, R:E, 0:C] = jnp.where(inside, DIFFUSION - rows, 0.0)
            c[2 * i + 1, R:E, 0:C] = jnp.where(inside, DIFFUSION + rows, 0.0)
            ends = side(ends_all, 3 + i)
            less, more = DIFFUSION - ends, DIFFUSION + ends
            c[2 * i, 0:R, C:] = less[0:R]
            c[2 * i + 1, 0:R, C:] = more[0:R]
            c[2 * i, R:E, C:] = jnp.where(inside[:, 0:128], less[R:E], 0.0)
            c[2 * i + 1, R:E, C:] = jnp.where(inside[:, 0:128], more[R:E], 0.0)

    unpack(got_rows_own, own_cols, x_ext, coef)
    c_all = [coef[i] for i in range(4)]
    state = tangent([x_ext[f] for f in range(3)], c_all, mix)
    for f in range(3):
        t_ext[f] = state[f]
    state = tangent([t_ext[f] for f in range(3)], c_all, mix)

    ring = jnp.zeros((R, 128), F32)
    for f in range(3):
        t_ext[f] = state[f]
        ends = jnp.where(lane < 64, t_ext[f, 0:R, 0:128], t_ext[f, 0:R, C - 128 : C])
        ring = jnp.where((lane >= 8 * f) & (lane < 8 * f + 8), rolled(ends, 8 * f + 4, 1), ring)
    edges = [jnp.where(sub < 4, t_ext[f, 0:8, 0:C], t_ext[f, R - 8 : R, 0:C]) for f in range(3)]
    ring_r[0] = jnp.where((sub < 2) | (sub >= 6), edges[0], rolled(edges[1], 4, 0))
    ring_r[1] = edges[2]
    quarter = R // 4
    folded = ring[0:quarter]
    group = iota((quarter, 128), 1)
    for q in range(1, 4):
        folded = jnp.where(group >= 32 * q, rolled(ring[quarter * q : quarter * (q + 1)], 32 * q, 1), folded)
    ring_c[...] = folded

    @pl.when(to_next)
    def _():
        late[0].start()
        late[1].start()

    for f in range(3):
        w_ext[f, :, C:] = side(own_cols, 5 + f)
        w_ext[f, R:E, 0:C] = rolled(jnp.where(sub < 4, got_rows_own[0, f], got_rows_own[1, f]), 4, 0)

    arrive(1)
    far_cols = columns(got_cols.at[1], got_corner.at[1], True)

    for f in range(3):
        t, base = f // 2, 4 * (f % 2)
        south_rows, north_rows = got_rows_far[0, t], got_rows_far[1, t]
        inc_rows = jnp.where(sub < 4, rolled(north_rows, -base, 0), rolled(south_rows, base, 0))
        mw_rows = jnp.where(sub < 4, rolled(north_rows, -base - 2, 0), rolled(south_rows, base + 2, 0))
        mw_cols = side(far_cols, f)
        g_ext[f, R:E, 0:C] = w_ext[f, R:E, 0:C] + mw_rows
        h_ext[f, R:E, 0:C] = mw_rows * inc_rows
        g_ext[f, :, C:] = w_ext[f, :, C:] + mw_cols
        h_ext[f, :, C:] = mw_cols * side(far_cols, 3 + f)

    state = [g_ext[f] * t_ext[f] - h_ext[f] for f in range(3)]
    state = adjoint(state, c_all, mix)
    for f in range(3):
        h_ext[f] = state[f]
    state = adjoint([h_ext[f] for f in range(3)], c_all, mix)
    for f in range(3):
        h_ext[f, 0:R, 0:C] = state[f][0:R, 0:C]

    @pl.when(follower)
    def _():
        for copy in origin_own:
            copy.wait_recv()
        reaction = pltpu.make_async_copy(prev_rea, prev_rea_s, load_sem.at[6])
        reaction.start()
        for d in feeds:
            feed_message(d).wait_recv()
        for f in range(3):
            xp_ext[f, 0:R, 0:C] = prev_inc[f]
        for i in range(2):
            cp_ext[2 * i, 0:R, 0:C] = DIFFUSION - prev_wind[i]
            cp_ext[2 * i + 1, 0:R, 0:C] = DIFFUSION + prev_wind[i]
        unpack(prev_rows, columns(prev_cols, prev_corner, False), xp_ext, cp_ext)
        reaction.wait()
        prev_mix = [[prev_rea_s[f, 0, g] + (KEEP if f == g else 0.0) for g in range(3)] for f in range(3)]
        c_prev = [cp_ext[i] for i in range(4)]
        state = tangent([xp_ext[f] for f in range(3)], c_prev, prev_mix)
        for f in range(3):
            xp_ext[f] = state[f]
        state = tangent([xp_ext[f] for f in range(3)], c_prev, prev_mix)
        for f in range(3):
            got_fwd[f] = state[f][0:R, 0:C]

    @pl.when(from_prev)
    def _():
        first.wait_recv()
        late[0].wait_recv()
        late[1].wait_recv()
        folded = got_ring_c[...]
        ring = jnp.concatenate([rolled(folded, -32 * q, 1) for q in range(4)], axis=0)
        for f in range(3):
            rows = rolled(got_ring_r[f // 2], 4 * (f % 2), 0)
            got_fwd[f, 0:8] = jnp.where(sub < 2, rows, got_fwd[f, 0:8])
            got_fwd[f, R - 8 : R] = jnp.where(sub >= 6, rows, got_fwd[f, R - 8 : R])
            ends = rolled(ring, -8 * f - 4, 1)
            got_fwd[f, :, 0:128] = jnp.where(lane < 2, ends, got_fwd[f, :, 0:128])
            got_fwd[f, :, C - 128 : C] = jnp.where(lane >= 126, ends, got_fwd[f, :, C - 128 : C])

    for f in range(3):
        out_ref[0, f] = mw_v[f] * (x_ext[f, 0:R, 0:C] - got_fwd[f]) + h_ext[f, 0:R, 0:C]

    for dw in range(2):
        for d, ok, _ in copies(dw):

            @pl.when(ok)
            def _(d=d, dw=dw):
                message(d, dw).wait_send()

    @pl.when(to_next)
    def _():
        first.wait_send()
        late[0].wait_send()
        late[1].wait_send()

    for d, feed in feeds.items():

        @pl.when(feed)
        def _(d=d):
            feed_message(d).wait_send()

    @pl.when(origin & has_next)
    def _():
        for copy in origin_own:
            copy.wait_send()

    @pl.when(has_prev)
    def _():
        bulk[0].wait_send()
        bulk[1].wait_send()


def per_device(sizes, *args):
    args = args[:3] + (jnp.transpose(args[3], (1, 0, 2)),) + args[4:]
    R, C = args[0].shape[-2:]
    count = args[4].shape[-1]
    args = [pltpu.with_memory_space_constraint(a, pltpu.HBM) for a in args]
    ext = (R + 8, C + 128)
    vmem = lambda *shape: pltpu.VMEM(shape, F32)
    anywhere = pl.BlockSpec(memory_space=pl.ANY)
    return pl.pallas_call(
        functools.partial(kernel, sizes),
        out_shape=jax.ShapeDtypeStruct(args[0].shape, F32),
        in_specs=[anywhere] * 6,
        out_specs=pl.BlockSpec(memory_space=pltpu.VMEM),
        scratch_shapes=[
            vmem(3, *ext), vmem(2, *ext), vmem(3, *ext), vmem(4, *ext), vmem(3, *ext), vmem(3, *ext), vmem(3, *ext),
            vmem(3, R, C), pltpu.SMEM((3, 1, 3), F32), pltpu.VMEM((1, count), jnp.int32), vmem(3, 1, count),
            vmem(R, 128), vmem(2, 2, R // 4, 128), vmem(2, 3, 8, C), vmem(2, 2, 8, C),
            vmem(3, R, C), vmem(2, 8, C), vmem(R // 4, 128),
            vmem(2, 3, 8, C), vmem(2, 2, 8, C), vmem(2, 2, R // 4, 128), vmem(2, 4, 8, 128),
            vmem(3, R, C), vmem(3, R, C), vmem(3, R, C), vmem(2, 8, C), vmem(R // 4, 128),
            pltpu.SemaphoreType.DMA((7,)), pltpu.SemaphoreType.DMA((2, 8)), pltpu.SemaphoreType.DMA((2, 8)),
            pltpu.SemaphoreType.DMA((8,)), pltpu.SemaphoreType.DMA((8,)), pltpu.SemaphoreType.DMA((8,)), pltpu.SemaphoreType.DMA((8,)),
            pltpu.SemaphoreType.REGULAR, pltpu.SemaphoreType.REGULAR,
            vmem(2, 3, 8, C), vmem(2, R // 4, 128), vmem(4, 8, 128), vmem(3, R, C), vmem(2, R, C), vmem(3, 1, 3),
            pltpu.SMEM((3, 1, 3), F32), vmem(3, *ext), vmem(4, *ext),
        ],
        compiler_params=pltpu.CompilerParams(
            collective_id=0, has_side_effects=True, vmem_limit_bytes=32 * 1024 * 1024
        ),
        cost_estimate=pl.CostEstimate(flops=10_000_000, bytes_accessed=1_000_000, transcendentals=0),
        name="window_product",
    )(*args)


def solution(mesh):
    sizes = tuple(mesh.shape[name] for name in ("win", "lat", "lon"))
    in_specs = (
        P("win", None, "lat", "lon"),
        P("win", None, "lat", "lon"),
        P("win", None, "lat", "lon"),
        P("win", None, None),
        P("win", "lat", "lon", None),
        P("win", None, "lat", "lon", None),
    )
    out_specs = P("win", None, "lat", "lon")
    return jax.shard_map(
        functools.partial(per_device, sizes), mesh=mesh, in_specs=in_specs, out_specs=out_specs, check_vma=False
    )
```

```python
import functools

import jax
import jax.numpy as jnp
from jax import lax
from jax.experimental import pallas as pl
from jax.experimental.pallas import tpu as pltpu
from jax.sharding import PartitionSpec as P

DIFFUSION = 0.15
KEEP = 1.0 - 4.0 * DIFFUSION
MESH = pl.DeviceIdType.MESH
F32 = jnp.float32
BF16 = jnp.bfloat16
DIRS = ((1, 0), (-1, 0), (0, 1), (0, -1), (1, 1), (1, -1), (-1, 1), (-1, -1))


def rolled(x, shift, axis):
    shift = shift % x.shape[axis]
    return x if shift == 0 else pltpu.roll(x, shift, axis)


def east(x):
    return rolled(x, -1, 1)


def west(x):
    return rolled(x, 1, 1)


def north(x):
    return rolled(x, -1, 0)


def south(x):
    return rolled(x, 1, 0)


def tangent(xs, coef, mix):
    a, b, c, d = coef
    out = []
    for f in range(3):
        x = xs[f]
        y = a * east(x) + b * west(x) + c * north(x) + d * south(x)
        out.append(y + mix[f][0] * xs[0] + mix[f][1] * xs[1] + mix[f][2] * xs[2])
    return out


def adjoint(zs, coef, mix):
    a, b, c, d = coef
    out = []
    for f in range(3):
        z = zs[f]
        y = east(b * z) + west(a * z) + north(d * z) + south(c * z)
        out.append(y + mix[0][f] * zs[0] + mix[1][f] * zs[1] + mix[2][f] * zs[2])
    return out


def iota(shape, axis):
    return lax.broadcasted_iota(jnp.int32, shape, axis)


def kernel(
    sizes,
    inc_h, mw_h, winds_h, rea_h, cells_h, ow_h,
    out_ref,
    x_ext, u_ext, w_ext, coef, g_ext, h_ext, t_ext,
    mw_v, rea_s, cells_v, ow_v,
    pack, cols, rows_own, rows_far, fwd0, ring_r, ring_c,
    got_rows_own, got_rows_far, got_cols, got_corner, inc_n, mw_n, got_fwd, got_ring_r, got_ring_c,
    load_sem, send_sem, recv_sem, xsend_sem, xrecv_sem, fsend_sem, frecv_sem, gate, far_ok,
    prev_rows, prev_cols, prev_corner, prev_inc, prev_wind, prev_rea, prev_rea_s, xp_ext, cp_ext,
):
    n_win, n_lat, n_lon = sizes
    win, lat, lon = lax.axis_index("win"), lax.axis_index("lat"), lax.axis_index("lon")
    R, C = 64, 256

    def lon_at(step):
        return lax.rem(lon + step + n_lon, n_lon)

    def lat_ok(step):
        return (lat + step >= 0) & (lat + step < n_lat)

    has_prev, has_next = win > 0, win < n_win - 1
    mid = n_lat // 2

    def is_last(at_lat, at_lon):
        return (at_lat == mid - 1) & (at_lon == n_lon - 1)

    def is_first(at_lat, at_lon):
        return (at_lat == mid) & (at_lon == 0)

    def is_corner(at_lat, at_lon):
        return (at_lat == mid) & (at_lon == n_lon - 1)

    def meets_origin(at_win, at_lat, at_lon):
        return (at_win < 2) & (at_lat < 2) & (at_lon == n_lon - 1)

    def deferred(at_win, at_lat, at_lon, d, dw):
        dlat, dlon = DIRS[d]
        held = lat < 0
        if dlat == 1 and dlon <= 0:
            held = held | is_last(at_lat, at_lon)
        if dlon == -1 and dlat >= 0:
            held = held | is_first(at_lat, at_lon)
        if (dlat == -1 and dlon <= 0) or (dlon == 1 and dlat >= 0):
            held = held | is_corner(at_lat, at_lon)
        if dlon == 1 and dlat <= 0:
            held = held | ((at_win == dw) & (at_lat == -dlat) & (at_lon == n_lon - 1))
        return held

    def answered(at_win, at_lat, at_lon, d):
        dlat, dlon = DIRS[d]
        early = lat < 0
        if dlon == -1:
            early = early | ((at_lon == 0) & (at_lat < mid) & (at_lat + dlat < mid))
        if dlat == 1:
            early = early | ((at_lat == mid - 1) & (at_lon < n_lon // 2))
        return early & ((at_win > 0) | (at_lat > 0) | (at_lon > 0))

    def turn(d):
        dlat, dlon = DIRS[d]
        urgent = later = lat < 0
        if dlat == -1:
            urgent = urgent | (lat == mid)
        if dlon == 1:
            urgent = urgent | (lon == n_lon - 1)
        if dlat == 1:
            later = later | (lat == mid - 1)
        if dlon == -1:
            later = later | (lon == 0)
        return jnp.where(urgent, 0, jnp.where(later, 2, 1))

    tile = (slice(None), pl.ds(0, R), pl.ds(0, C))
    loads = [
        pltpu.make_async_copy(cells_h.at[0, 0], cells_v, load_sem.at[0]),
        pltpu.make_async_copy(ow_h.at[0, :, 0], ow_v, load_sem.at[1]),
        pltpu.make_async_copy(inc_h.at[0], x_ext.at[tile], load_sem.at[2]),
        pltpu.make_async_copy(winds_h.at[0], u_ext.at[tile], load_sem.at[3]),
        pltpu.make_async_copy(mw_h.at[0], mw_v, load_sem.at[4]),
        pltpu.make_async_copy(rea_h, rea_s, load_sem.at[5]),
    ]
    for load in loads:
        load.start()

    barrier = pltpu.get_barrier_semaphore()

    def tell(ok, target):
        @pl.when(ok)
        def _():
            pl.semaphore_signal(barrier, inc=1, device_id=target, device_id_type=MESH)

    for d, (dlat, dlon) in enumerate(DIRS):
        for dw in range(2):
            source = (win + dw, lat - dlat, lon_at(-dlon))
            ok = lat_ok(-dlat) & jnp.logical_not(deferred(*source, d, dw) | answered(*source, d))
            tell(ok & has_next if dw else ok, source)
        tell(has_prev & lat_ok(dlat) & answered(win, lat, lon, d), (win - 1, lat + dlat, lon_at(dlon)))
    origin = (win == 0) & (lat == 0) & (lon == 0)
    follower = (win == 1) & (lat == 0) & (lon == 0)
    feeds = {
        d: has_next & (win == 0) & (lat == -dlat) & (lon_at(dlon) == 0)
        for d, (dlat, dlon) in enumerate(DIRS)
        if dlat <= 0
    }
    for d in feeds:
        tell(follower, (win - 1, lat - DIRS[d][0], lon_at(-DIRS[d][1])))
    tell(origin, (win, lat, lon_at(-2)))
    tell(origin & has_next, (win + 1, lat, lon_at(-2)))
    tell(has_next, (win + 1, lat, lon))
    tell(has_prev, (win - 1, lat, lon))

    for d, (dlat, dlon) in enumerate(DIRS):
        for dw in range(2):
            there = lat_ok(-dlat) & (has_next if dw else (win >= 0))

            @pl.when(jnp.logical_not(there))
            def _(d=d, dw=dw, dlat=dlat, dlon=dlon):
                if dlon == 0:
                    ref = got_rows_far.at[d] if dw else got_rows_own.at[d]
                elif dlat == 0:
                    ref = got_cols.at[dw, d - 2]
                else:
                    ref = got_corner.at[dw, d - 4]
                ref[...] = jnp.zeros(ref.shape, F32)

    @pl.when(follower)
    def _():
        prev_rows[0] = jnp.zeros(prev_rows.shape[1:], F32)
        for i, (dlat, _) in enumerate(DIRS[4:]):
            if dlat > 0:
                prev_corner[i] = jnp.zeros(prev_corner.shape[1:], F32)

    @pl.when(jnp.logical_not(has_next))
    def _():
        inc_n[...] = jnp.zeros(inc_n.shape, F32)
        mw_n[...] = jnp.zeros(mw_n.shape, F32)

    @pl.when(jnp.logical_not(has_prev))
    def _():
        got_fwd[...] = jnp.zeros(got_fwd.shape, F32)

    loads[0].wait()
    loads[1].wait()
    cells = cells_v[...]
    count = cells.shape[1]
    row_of = lax.shift_right_logical(cells, 8)
    col_of = lax.bitwise_and(cells, 255)
    at_row = iota((R, count), 0) == row_of
    at_col = jnp.where(iota((C, count), 0) == col_of, 1.0, 0.0).astype(BF16)
    spread = []
    for f in range(3):
        rest = ow_v[f]
        for _ in range(3):
            part = rest.astype(BF16).astype(F32)
            rest = rest - part
            spread.append(jnp.where(at_row, part, 0.0).astype(BF16))
    sums = lax.dot_general(
        jnp.concatenate(spread, axis=0), at_col, (((1,), (1,)), ((), ())), preferred_element_type=F32
    )
    for f in range(3):
        top, low, rest = (sums[R * (3 * f + p) : R * (3 * f + p + 1)] for p in range(3))
        w_ext[f, 0:R, 0:C] = top + low + rest

    for load in loads[2:]:
        load.wait()
    mix = [[rea_s[f, 0, g] + (KEEP if f == g else 0.0) for g in range(3)] for f in range(3)]

    sub = iota((8, C), 0)
    lu, lv = u_ext[0, R - 8 : R, 0:C], u_ext[1, R - 8 : R, 0:C]
    fu, fv = u_ext[0, 0:8, 0:C], u_ext[1, 0:8, 0:C]
    for f in range(3):
        wind = jnp.where(sub == 1, rolled(lv, -4 - f, 0), rolled(lu, -5 - f, 0))
        obs = rolled(w_ext[f, R - 8 : R, 0:C], 4, 0)
        rows_own[0, f] = jnp.where(sub >= 4, x_ext[f, R - 8 : R, 0:C], jnp.where(sub >= 2, obs, wind))
        wind = jnp.where(sub == 6, rolled(fu, 6 - f, 0), rolled(fv, 7 - f, 0))
        obs = rolled(w_ext[f, 0:8, 0:C], 4, 0)
        rows_own[1, f] = jnp.where(sub < 4, x_ext[f, 0:8, 0:C], jnp.where(sub < 6, obs, wind))
    for pair in range(2):
        n_rows = n_cols = None
        for f in range(2 * pair, min(3, 2 * pair + 2)):
            base = 4 * (f % 2)
            lx, lm = x_ext[f, R - 8 : R, 0:C], mw_v[f, R - 8 : R, 0:C]
            fx, fm = x_ext[f, 0:8, 0:C], mw_v[f, 0:8, 0:C]
            top = jnp.where(lax.rem(sub, 4) >= 2, rolled(lx, -base, 0), rolled(lm, -base - 2, 0))
            bottom = jnp.where(lax.rem(sub, 4) < 2, rolled(fx, base, 0), rolled(fm, base + 2, 0))
            n_rows = top if n_rows is None else jnp.where(sub < 4, top, n_rows)
            n_cols = bottom if n_cols is None else jnp.where(sub >= 4, bottom, n_cols)
        rows_far[0, pair] = n_rows
        rows_far[1, pair] = n_cols

    lane = iota((R, 128), 1)
    packed = jnp.zeros((R, 128), F32)
    own = [(x_ext, 0), (x_ext, 1), (x_ext, 2), (u_ext, 0), (u_ext, 1), (w_ext, 0), (w_ext, 1), (w_ext, 2), (mw_v, 0), (mw_v, 1), (mw_v, 2), (x_ext, 0), (x_ext, 1), (x_ext, 2)]
    for a, (ref, f) in enumerate(own):
        ends = jnp.where(lane < 64, ref[f, 0:R, 0:128], ref[f, 0:R, C - 128 : C])
        packed = jnp.where((lane >= 8 * a) & (lane < 8 * a + 8), rolled(ends, 8 * a + 4, 1), packed)
    pack[...] = packed
    half = R // 2
    low_lane = lax.rem(iota((half, 128), 1), 8) < 4
    left = iota((half // 2, 128), 1) < 64
    for e, pair in enumerate((
        jnp.where(low_lane, packed[:half], rolled(packed[half:], 4, 1)),
        jnp.where(low_lane, rolled(packed[half:], -4, 1), packed[:half]),
    )):
        upper, lower = pair[: half // 2], pair[half // 2 :]
        cols[0, e] = jnp.where(left, upper, rolled(lower, 64, 1))
        cols[1, e] = jnp.where(left, rolled(upper, 64, 1), lower)

    lats = 1 + lat_ok(1).astype(jnp.int32) + lat_ok(-1).astype(jnp.int32)
    prev, nxt = has_prev.astype(jnp.int32), has_next.astype(jnp.int32)
    ends = (is_last(lat, lon) | is_first(lat, lon)).astype(jnp.int32)
    meets = meets_origin(win, lat, lon).astype(jnp.int32)
    knows_origin = (win < 2) & (lat == 0) & (lon == n_lon - 2)
    asks = owed = jnp.int32(0)
    for d, (dlat, dlon) in enumerate(DIRS):
        asks += (lat_ok(dlat) & answered(win, lat, lon, d)).astype(jnp.int32)
        owed += (lat_ok(-dlat) & answered(win + 1, lat - dlat, lon_at(-dlon), d)).astype(jnp.int32)
    fed = functools.reduce(jnp.add, [feed.astype(jnp.int32) for feed in feeds.values()])
    corner = is_corner(lat, lon).astype(jnp.int32)
    others = (3 * lats - 2 * ends - 4 * corner - asks) * (1 + prev) - 1 + nxt + owed * nxt
    pl.semaphore_wait(barrier, others - meets + knows_origin.astype(jnp.int32) + fed)

    def feed_message(d):
        dlat, dlon = DIRS[d]
        if dlon == 0:
            src, dst = rows_own.at[d], prev_rows.at[d]
        elif dlat == 0:
            src, dst = cols.at[0, d - 2], prev_cols.at[d - 2]
        else:
            src, dst = pack.at[pl.ds(R - 8 if dlat == 1 else 0, 8)], prev_corner.at[d - 4]
        return pltpu.make_async_remote_copy(
            src_ref=src,
            dst_ref=dst,
            send_sem=fsend_sem.at[d],
            recv_sem=frecv_sem.at[d],
            device_id=(win + 1, lat + dlat, lon_at(dlon)),
            device_id_type=MESH,
        )

    def message(d, dw):
        dlat, dlon = DIRS[d]
        if dlon == 0:
            src, dst = (rows_far.at[d], got_rows_far.at[d]) if dw else (rows_own.at[d], got_rows_own.at[d])
        elif dlat == 0:
            src, dst = cols.at[dw, d - 2], got_cols.at[dw, d - 2]
        else:
            src, dst = pack.at[pl.ds(R - 8 if dlat == 1 else 0, 8)], got_corner.at[dw, d - 4]
        return pltpu.make_async_remote_copy(
            src_ref=src,
            dst_ref=dst,
            send_sem=send_sem.at[dw, d],
            recv_sem=recv_sem.at[dw, d],
            device_id=(win - dw, lat + dlat, lon_at(dlon)),
            device_id_type=MESH,
        )

    def across(i, src, dst, step):
        return pltpu.make_async_remote_copy(
            src_ref=src,
            dst_ref=dst,
            send_sem=xsend_sem.at[i],
            recv_sem=xrecv_sem.at[i],
            device_id=(win + step, lat, lon),
            device_id_type=MESH,
        )

    def copies(dw):
        for d, (dlat, _) in enumerate(DIRS):
            yield d, lat_ok(dlat) & (has_prev if dw else (win >= 0)), lat_ok(-dlat) & (has_next if dw else (win >= 0))

    def answer():
        for dw in range(2):
            for d, _, ok in copies(dw):
                dlat, dlon = DIRS[d]
                source = (win + dw, lat - dlat, lon_at(-dlon))


                @pl.when(ok & answered(*source, d))
                def _(source=source):
                    pl.semaphore_signal(far_ok, inc=1, device_id=source, device_id_type=MESH)

    for now in range(3):
        for dw in range(2):
            for d, ok, _ in copies(dw):

                @pl.when(ok & (turn(d) == now) & jnp.logical_not(deferred(win, lat, lon, d, dw) | answered(win, lat, lon, d)))
                def _(d=d, dw=dw):
                    message(d, dw).start()

        if now == 0:
            answer()

    bulk = [across(0, inc_h.at[0], inc_n, -1), across(1, mw_h.at[0], mw_n, -1)]
    first = across(2, fwd0, got_fwd, 1)
    late = [across(3, ring_r, got_ring_r, 1), across(4, ring_c, got_ring_c, 1)]
    origin_own = [across(5, inc_h.at[0], prev_inc, 1), across(6, winds_h.at[0], prev_wind, 1), across(7, rea_h, prev_rea, 1)]
    to_next = has_next & jnp.logical_not(origin)
    from_prev = has_prev & jnp.logical_not(follower)

    for d, feed in feeds.items():

        @pl.when(feed)
        def _(d=d):
            feed_message(d).start()

    @pl.when(origin & has_next)
    def _():
        for copy in origin_own:
            copy.start()

    @pl.when(((lat == mid - 1) | (lat == mid)) & (lon == n_lon - 2))
    def _():
        pl.semaphore_signal(gate, inc=1, device_id=(win, lat, lon + 1), device_id_type=MESH)

    @pl.when(knows_origin)
    def _():
        pl.semaphore_signal(gate, inc=1, device_id=(win, lat, lon + 1), device_id_type=MESH)
        pl.semaphore_signal(gate, inc=1, device_id=(win, lat + 1, lon + 1), device_id_type=MESH)

    @pl.when((lat == mid + 1) & ((lon == 0) | (lon == n_lon - 1)))
    def _():
        pl.semaphore_signal(gate, inc=1, device_id=(win, lat - 1, lon), device_id_type=MESH)

    uc, vc = u_ext[0, 0:R, 0:C], u_ext[1, 0:R, 0:C]
    coef[0, 0:R, 0:C] = DIFFUSION - uc
    coef[1, 0:R, 0:C] = DIFFUSION + uc
    coef[2, 0:R, 0:C] = DIFFUSION - vc
    coef[3, 0:R, 0:C] = DIFFUSION + vc
    c_tile = [coef[i, 0:R, 0:C] for i in range(4)]
    state = [x_ext[f, 0:R, 0:C] for f in range(3)]
    for _ in range(2):
        state = tangent(state, c_tile, mix)
    for f in range(3):
        fwd0[f] = state[f]

    @pl.when(to_next)
    def _():
        first.start()

    @pl.when(has_prev)
    def _():
        bulk[0].start()
        bulk[1].start()

    @pl.when(ends + meets + corner > 0)
    def _():
        pl.semaphore_wait(gate, ends + meets + 2 * corner)
        for dw in range(2):
            for d, ok, _ in copies(dw):

                @pl.when(ok & deferred(win, lat, lon, d, dw))
                def _(d=d, dw=dw):
                    message(d, dw).start()

    @pl.when(asks > 0)
    def _():
        pl.semaphore_wait(far_ok, asks * (1 + prev))
        for dw in range(2):
            for d, ok, _ in copies(dw):

                @pl.when(ok & answered(win, lat, lon, d))
                def _(d=d, dw=dw):
                    message(d, dw).start()

    def arrive(dw):
        for d, _, ok in copies(dw):

            @pl.when(ok)
            def _(d=d, dw=dw):
                message(d, dw).wait_recv()

    arrive(0)

    corner_low = lax.rem(iota((8, 128), 1), 8) < 4
    corner_sub = iota((8, 128), 0)

    def columns(from_cols, from_corner, far):
        from_west, from_east = (
            jnp.concatenate([from_cols[i], rolled(from_cols[i], 64, 1)], axis=0) for i in range(2)
        )
        upper = jnp.where(low_lane, from_west, from_east)
        lower = jnp.where(low_lane, rolled(from_west, -4, 1), rolled(from_east, 4, 1))
        sw, se, nw, ne = (from_corner[i] for i in range(4))
        rim = jnp.where(corner_sub < 4, jnp.where(corner_low, nw, ne), jnp.where(corner_low, sw, se))
        return jnp.concatenate([upper, lower, rolled(rim, 64, 1) if far else rim], axis=0)

    own_cols = columns(got_cols.at[0], got_corner.at[0], False)

    def side(ends, a):
        return rolled(ends, -8 * a - 4, 1)

    E = R + 8
    inside = jnp.where(iota((8, C), 0) < 4, lat_ok(1).astype(F32), lat_ok(-1).astype(F32)) > 0.0
    def unpack(from_rows, ends_all, x, c):
        for f in range(3):
            x[f, :, C:] = side(ends_all, f)
            x[f, R:E, 0:C] = jnp.where(sub < 4, from_rows[1, f], from_rows[0, f])
        for i in range(2):
            rows = jnp.zeros((8, C), F32)
            for t in range(3):
                rows = jnp.where(sub == t, rolled(from_rows[1, t], t - 6 - i, 0), rows)
                rows = jnp.where(sub == 5 + t, rolled(from_rows[0, t], 5 + t - i, 0), rows)
            c[2 * i, R:E, 0:C] = jnp.where(inside, DIFFUSION - rows, 0.0)
            c[2 * i + 1, R:E, 0:C] = jnp.where(inside, DIFFUSION + rows, 0.0)
            ends = side(ends_all, 3 + i)
            less, more = DIFFUSION - ends, DIFFUSION + ends
            c[2 * i, 0:R, C:] = less[0:R]
            c[2 * i + 1, 0:R, C:] = more[0:R]
            c[2 * i, R:E, C:] = jnp.where(inside[:, 0:128], less[R:E], 0.0)
            c[2 * i + 1, R:E, C:] = jnp.where(inside[:, 0:128], more[R:E], 0.0)

    unpack(got_rows_own, own_cols, x_ext, coef)
    for f in range(3):
        w_ext[f, :, C:] = side(own_cols, 5 + f)
        w_ext[f, R:E, 0:C] = rolled(jnp.where(sub < 4, got_rows_own[0, f], got_rows_own[1, f]), 4, 0)

    c_all = [coef[i] for i in range(4)]
    state = tangent([x_ext[f] for f in range(3)], c_all, mix)
    for f in range(3):
        t_ext[f] = state[f]
    state = tangent([t_ext[f] for f in range(3)], c_all, mix)

    ring = jnp.zeros((R, 128), F32)
    for f in range(3):
        t_ext[f] = state[f]
        ring_r[f] = jnp.where(sub < 4, t_ext[f, 0:8, 0:C], t_ext[f, R - 8 : R, 0:C])
        ends = jnp.where(lane < 64, t_ext[f, 0:R, 0:128], t_ext[f, 0:R, C - 128 : C])
        ring = jnp.where((lane >= 8 * f) & (lane < 8 * f + 8), rolled(ends, 8 * f + 4, 1), ring)
    quarter = R // 4
    folded = ring[0:quarter]
    group = iota((quarter, 128), 1)
    for q in range(1, 4):
        folded = jnp.where(group >= 32 * q, rolled(ring[quarter * q : quarter * (q + 1)], 32 * q, 1), folded)
    ring_c[...] = folded

    @pl.when(to_next)
    def _():
        late[0].start()
        late[1].start()

    arrive(1)
    far_cols = columns(got_cols.at[1], got_corner.at[1], True)

    @pl.when(has_next)
    def _():
        bulk[0].wait_recv()
        bulk[1].wait_recv()

    for f in range(3):
        t, base = f // 2, 4 * (f % 2)
        south_rows, north_rows = got_rows_far[0, t], got_rows_far[1, t]
        inc_rows = jnp.where(sub < 4, rolled(north_rows, -base, 0), rolled(south_rows, base, 0))
        mw_rows = jnp.where(sub < 4, rolled(north_rows, -base - 2, 0), rolled(south_rows, base + 2, 0))
        mw_cols = side(far_cols, f)
        g_ext[f, 0:R, 0:C] = w_ext[f, 0:R, 0:C] + mw_n[f]
        h_ext[f, 0:R, 0:C] = mw_n[f] * inc_n[f]
        g_ext[f, R:E, 0:C] = w_ext[f, R:E, 0:C] + mw_rows
        h_ext[f, R:E, 0:C] = mw_rows * inc_rows
        g_ext[f, :, C:] = w_ext[f, :, C:] + mw_cols
        h_ext[f, :, C:] = mw_cols * side(far_cols, 3 + f)

    state = [g_ext[f] * t_ext[f] - h_ext[f] for f in range(3)]
    state = adjoint(state, c_all, mix)
    for f in range(3):
        h_ext[f] = state[f]
    state = adjoint([h_ext[f] for f in range(3)], c_all, mix)
    for f in range(3):
        h_ext[f] = state[f]

    @pl.when(follower)
    def _():
        for copy in origin_own:
            copy.wait_recv()
        reaction = pltpu.make_async_copy(prev_rea, prev_rea_s, load_sem.at[6])
        reaction.start()
        for d in feeds:
            feed_message(d).wait_recv()
        for f in range(3):
            xp_ext[f, 0:R, 0:C] = prev_inc[f]
        for i in range(2):
            cp_ext[2 * i, 0:R, 0:C] = DIFFUSION - prev_wind[i]
            cp_ext[2 * i + 1, 0:R, 0:C] = DIFFUSION + prev_wind[i]
        unpack(prev_rows, columns(prev_cols, prev_corner, False), xp_ext, cp_ext)
        reaction.wait()
        prev_mix = [[prev_rea_s[f, 0, g] + (KEEP if f == g else 0.0) for g in range(3)] for f in range(3)]
        c_prev = [cp_ext[i] for i in range(4)]
        state = tangent([xp_ext[f] for f in range(3)], c_prev, prev_mix)
        for f in range(3):
            xp_ext[f] = state[f]
        state = tangent([xp_ext[f] for f in range(3)], c_prev, prev_mix)
        for f in range(3):
            got_fwd[f] = state[f][0:R, 0:C]

    @pl.when(from_prev)
    def _():
        first.wait_recv()
        late[0].wait_recv()
        late[1].wait_recv()
        folded = got_ring_c[...]
        ring = jnp.concatenate([rolled(folded, -32 * q, 1) for q in range(4)], axis=0)
        for f in range(3):
            rows = got_ring_r[f]
            got_fwd[f, 0:8] = jnp.where(sub < 2, rows, got_fwd[f, 0:8])
            got_fwd[f, R - 8 : R] = jnp.where(sub >= 6, rows, got_fwd[f, R - 8 : R])
            ends = rolled(ring, -8 * f - 4, 1)
            got_fwd[f, :, 0:128] = jnp.where(lane < 2, ends, got_fwd[f, :, 0:128])
            got_fwd[f, :, C - 128 : C] = jnp.where(lane >= 126, ends, got_fwd[f, :, C - 128 : C])

    for f in range(3):
        out_ref[0, f] = mw_v[f] * (x_ext[f, 0:R, 0:C] - got_fwd[f]) + h_ext[f, 0:R, 0:C]

    for dw in range(2):
        for d, ok, _ in copies(dw):

            @pl.when(ok)
            def _(d=d, dw=dw):
                message(d, dw).wait_send()

    @pl.when(to_next)
    def _():
        first.wait_send()
        late[0].wait_send()
        late[1].wait_send()

    for d, feed in feeds.items():

        @pl.when(feed)
        def _(d=d):
            feed_message(d).wait_send()

    @pl.when(origin & has_next)
    def _():
        for copy in origin_own:
            copy.wait_send()

    @pl.when(has_prev)
    def _():
        bulk[0].wait_send()
        bulk[1].wait_send()


def per_device(sizes, *args):
    args = args[:3] + (jnp.transpose(args[3], (1, 0, 2)),) + args[4:]
    R, C = args[0].shape[-2:]
    count = args[4].shape[-1]
    args = [pltpu.with_memory_space_constraint(a, pltpu.HBM) for a in args]
    ext = (R + 8, C + 128)
    vmem = lambda *shape: pltpu.VMEM(shape, F32)
    anywhere = pl.BlockSpec(memory_space=pl.ANY)
    return pl.pallas_call(
        functools.partial(kernel, sizes),
        out_shape=jax.ShapeDtypeStruct(args[0].shape, F32),
        in_specs=[anywhere] * 6,
        out_specs=pl.BlockSpec(memory_space=pltpu.VMEM),
        scratch_shapes=[
            vmem(3, *ext), vmem(2, *ext), vmem(3, *ext), vmem(4, *ext), vmem(3, *ext), vmem(3, *ext), vmem(3, *ext),
            vmem(3, R, C), pltpu.SMEM((3, 1, 3), F32), pltpu.VMEM((1, count), jnp.int32), vmem(3, 1, count),
            vmem(R, 128), vmem(2, 2, R // 4, 128), vmem(2, 3, 8, C), vmem(2, 2, 8, C),
            vmem(3, R, C), vmem(3, 8, C), vmem(R // 4, 128),
            vmem(2, 3, 8, C), vmem(2, 2, 8, C), vmem(2, 2, R // 4, 128), vmem(2, 4, 8, 128),
            vmem(3, R, C), vmem(3, R, C), vmem(3, R, C), vmem(3, 8, C), vmem(R // 4, 128),
            pltpu.SemaphoreType.DMA((7,)), pltpu.SemaphoreType.DMA((2, 8)), pltpu.SemaphoreType.DMA((2, 8)),
            pltpu.SemaphoreType.DMA((8,)), pltpu.SemaphoreType.DMA((8,)), pltpu.SemaphoreType.DMA((8,)), pltpu.SemaphoreType.DMA((8,)),
            pltpu.SemaphoreType.REGULAR, pltpu.SemaphoreType.REGULAR,
            vmem(2, 3, 8, C), vmem(2, R // 4, 128), vmem(4, 8, 128), vmem(3, R, C), vmem(2, R, C), vmem(3, 1, 3),
            pltpu.SMEM((3, 1, 3), F32), vmem(3, *ext), vmem(4, *ext),
        ],
        compiler_params=pltpu.CompilerParams(
            collective_id=0, has_side_effects=True, vmem_limit_bytes=32 * 1024 * 1024
        ),
        cost_estimate=pl.CostEstimate(flops=10_000_000, bytes_accessed=1_000_000, transcendentals=0),
        name="window_product",
    )(*args)


def solution(mesh):
    sizes = tuple(mesh.shape[name] for name in ("win", "lat", "lon"))
    in_specs = (
        P("win", None, "lat", "lon"),
        P("win", None, "lat", "lon"),
        P("win", None, "lat", "lon"),
        P("win", None, None),
        P("win", "lat", "lon", None),
        P("win", None, "lat", "lon", None),
    )
    out_specs = P("win", None, "lat", "lon")
    return jax.shard_map(
        functools.partial(per_device, sizes), mesh=mesh, in_specs=in_specs, out_specs=out_specs, check_vma=False
    )
```
